256 devices in a mesh: dp: 16 (over z, core), tensor: 16 (over y, x).
Axes of the slice: x: 4, y: 4, z: 8, core: 2. Of those that a mesh axis runs over, the one named last changes fastest.
Arguments:
- tokens: bfloat16 [4096, 4096], P('dp'), may hold values from -30 to 30
- neighbour_buffer: bfloat16 [256, 128, 4096], P('dp', None, 'tensor'), may hold values from -6 to 6
- shard_ids: int32 [64, 2], P('dp'), may hold values from 0 to 15, as said below
- row_ids: int32 [64, 2], P('dp'), may hold values from 0 to 15
- query_weight: bfloat16 [4096, 2048], P(None, 'tensor'), may hold values from -0.09375 to 0.09375
- key_weight: bfloat16 [4096, 2048], P(None, 'tensor'), may hold values from -0.09375 to 0.09375
- value_weight: bfloat16 [4096, 2048], P(None, 'tensor'), may hold values from -0.09375 to 0.09375
- output_weight: bfloat16 [2048, 4096], P('tensor'), may hold values from -0.5 to 0.5
- up_weight: bfloat16 [4096, 8192], P('dp', 'tensor'), may hold values from -0.09375 to 0.09375
- down_weight: bfloat16 [8192, 4096], P('tensor', 'dp'), may hold values from -0.0625 to 0.0625
- grad_output: bfloat16 [4096, 4096], P('dp'), may hold values from -6 to 6
Outputs:
- layer_out: bfloat16 [4096, 4096], P(('dp', 'tensor'))
- grad_tokens: bfloat16 [4096, 4096], P(('dp', 'tensor'))
- query_grad: float32 [4096, 2048], P('dp', 'tensor')
- key_grad: float32 [4096, 2048], P('dp', 'tensor')
- value_grad: float32 [4096, 2048], P('dp', 'tensor')
- mix_grad: float32 [2048, 4096], P('tensor', 'dp')
The draws below stay inside these ranges and needn't reach their ends.
Inputs may be any that keep to these rules, and one draw needn't show every extreme that they name: `shard_ids`: A block's two neighbours lie in different shards. Among the 4 blocks of one index of dp no shard is named more than 2 times, and some shard is named exactly 2 times among the blocks of every index of dp.
All inputs are finite; a program needn't handle non-finite values.
Results may differ from the reference program's by a relative error of at most 0.034.
Values may be sent and summed in bfloat16 or wider, within the bound.
No kernel may reach another device: no remote copies, remote signals or barrier semaphores. Data moves between devices by JAX's collectives and lax.ppermute only.
A program may use at most 128 MiB of HBM per device.

```python
import math
import jax
import jax.numpy as jnp
from jax import lax

D = 4096
HEADS = 16
HD = 128
FF = 8192
BLOCK = 64
NLEN = 128
TOK_DEV = 256
BUF = 16
TOKENS = 4096
BLOCKS = 64
BLK_DEV = 4
N_DP = 16
N_TENSOR = 16


def draw_tokens(key, part):
    key = jax.random.fold_in(key, 11)
    key_base, key_cols, key_rows = jax.random.split(key, 3)
    base = jax.random.normal(key_base, (TOKENS, D), jnp.float32)
    spread = math.log(10.0)
    column_scale = jnp.exp(jax.random.uniform(key_cols, (1, D), jnp.float32, 0.0, spread))
    token_scale = jnp.exp(jax.random.uniform(key_rows, (TOKENS, 1), jnp.float32, 0.0, spread))
    return jnp.clip(base * column_scale * token_scale * 0.05, -30.0, 30.0).astype(jnp.bfloat16)


def draw_shard_ids(key, part):
    key = jax.random.fold_in(key, 23)
    key_hot, key_blocks = jax.random.split(key)
    capacity = BLK_DEV // 2
    others_count = N_DP - 1
    extra_slots = 2 * BLK_DEV - capacity
    hot_shard = jax.random.randint(key_hot, (), 0, N_DP)

    def one_device(device_key):
        key_perm, key_order, key_swap = jax.random.split(device_key, 3)
        shuffled = jax.random.permutation(key_perm, others_count)
        others = jnp.where(shuffled >= hot_shard, shuffled + 1, shuffled)
        filled = others[jnp.arange(extra_slots) % others_count]
        block_place = jnp.arange(BLK_DEV)
        second_col = filled[block_place]
        first_col = jnp.where(block_place < capacity, hot_shard, filled[block_place + capacity])
        paired = jnp.stack([first_col, second_col], axis=1)
        swap_flag = jax.random.randint(key_swap, (BLK_DEV, 1), 0, 2)
        paired = jnp.where(swap_flag == 1, paired[:, ::-1], paired)
        block_order = jax.random.permutation(key_order, BLK_DEV)
        return paired[block_order]
    device_keys = jax.random.split(key_blocks, N_DP)
    return jax.vmap(one_device)(device_keys).reshape(BLOCKS, 2).astype(jnp.int32)


def touch_ends(array, rng, smallest, high):
    extent = array.shape
    place = [jax.random.randint(jax.random.fold_in(rng, axis), (), 0, extent[axis]) for axis in range(len(extent))]
    array = array.at[tuple(place)].set(smallest)
    longest = extent.index(max(extent))
    place[longest] = (place[longest] + 1) % extent[longest]
    return array.at[tuple(place)].set(high)


def strengthened(array, key, source, target, blocks, factor):
    def block_of(axis_at):
        return (jnp.arange(array.shape[axis_at]) // (array.shape[axis_at] // blocks)).reshape((-1,) + (1,) * (array.ndim - 1 - axis_at))

    near = jax.random.permutation(key, blocks)[block_of(target)]
    far = (block_of(target) + blocks // 2) % blocks
    return jnp.where((block_of(source) == near) | (block_of(source) == far), factor * array, array)


def shard_levels(key, extent, cuts, low, largest):
    def one(position, blocks):
        draws = jax.random.uniform(jax.random.fold_in(jax.random.fold_in(key, 6), position), (blocks,), jnp.float32, low / len(cuts), largest / len(cuts))
        return jnp.repeat(jnp.exp(draws), extent[position] // blocks).reshape((-1,) + (1,) * (len(extent) - position - 1))

    gain = one(*cuts[0])
    for cut in cuts[1:]:
        gain = gain * one(*cut)
    return gain


def normal_values(key, shape, scale, reach, cuts=(), dtype=jnp.bfloat16):
    entries = scale * jax.random.normal(key, shape, jnp.float32)
    if cuts:
        entries = entries * shard_levels(key, shape, cuts, -0.22, 0.18)
    return jnp.clip(entries, -reach, reach).astype(dtype)


def noise_with(key, dims, scale, reach, pieces, heavy, dtype=jnp.bfloat16):
    drawn = scale * jax.random.normal(key, dims, jnp.float32)
    if pieces:
        drawn = drawn * shard_levels(key, dims, pieces, -0.22, 0.18)
    return jnp.clip(strengthened(drawn, jax.random.fold_in(key, 3), *heavy), -reach, reach).astype(dtype)


def setup_inputs(seed: int = 0) -> dict:
    streams_of = jax.random.split(jax.random.key(seed), 12)
    return {
        "tokens": draw_tokens(jax.random.fold_in(streams_of[11], 71), 0),
        "neighbour_buffer": normal_values(streams_of[1], (N_DP * BUF, NLEN, D), 1.0, 6.0, ((0, 16), (2, 16))),
        "shard_ids": draw_shard_ids(jax.random.fold_in(streams_of[11], 71), 0),
        "row_ids": touch_ends(jax.random.randint(streams_of[3], (BLOCKS, 2), 0, BUF), jax.random.fold_in(streams_of[3], 1), 0, BUF - 1).astype(jnp.int32),
        "query_weight": normal_values(streams_of[4], (D, HEADS * HD), D ** -0.5, 0.09375, ((1, 16),)),
        "key_weight": normal_values(streams_of[5], (D, HEADS * HD), D ** -0.5, 0.09375, ((1, 16),)),
        "value_weight": normal_values(streams_of[6], (D, HEADS * HD), D ** -0.5, 0.09375, ((1, 16),)),
        "output_weight": normal_values(streams_of[7], (HEADS * HD, D), HD ** -0.5, 0.5, ((0, 16),)),
        "up_weight": normal_values(streams_of[8], (D, FF), D ** -0.5, 0.09375, ((0, 16), (1, 16))),
        "down_weight": normal_values(streams_of[9], (FF, D), FF ** -0.5, 0.0625, ((0, 16), (1, 16))),
        "grad_output": noise_with(streams_of[10], (TOKENS, D), 1.0, 6.0, ((0, 16),), (0, 1, 16, 2.0)),
    }


epsilon = 1e-06
gelu_root = 0.7978845608028654
gelu_cubic = 0.044715

def rms_scale(values):
    return lax.rsqrt(lax.optimization_barrier(jnp.mean(values * values, axis=-1, keepdims=True)) + epsilon)

def norm_back(values, factor, incoming):
    normal_part = values * factor
    return (incoming - normal_part * lax.optimization_barrier(jnp.mean(incoming * normal_part, axis=-1, keepdims=True))) * factor

def gelu_value(inputs):
    inner = gelu_root * (inputs + gelu_cubic * inputs * inputs * inputs)
    return 0.5 * inputs * (1.0 + jnp.tanh(inner))

def gelu_slope(inputs):
    inner = gelu_root * (inputs + gelu_cubic * inputs * inputs * inputs)
    tanh_part = jnp.tanh(inner)
    return 0.5 * (1.0 + tanh_part) + 0.5 * inputs * (1.0 - tanh_part * tanh_part) * gelu_root * (1.0 + 3.0 * gelu_cubic * inputs * inputs)

def rounded(partial_value):
    return lax.optimization_barrier(partial_value.astype(jnp.bfloat16)).astype(jnp.float32)

def split_sum(left_side, right_side, group_width):
    running = jnp.zeros((left_side.shape[0], right_side.shape[1]), jnp.float32)
    for group_index in range(N_TENSOR):
        low_edge = group_index * group_width
        partial_value = jnp.dot(left_side[:, low_edge:low_edge + group_width], right_side[low_edge:low_edge + group_width], preferred_element_type=jnp.float32)
        running = running + rounded(partial_value)
    return running

def group_grad(left_side, right_side, group_rows):
    running = jnp.zeros((left_side.shape[1], right_side.shape[1]), jnp.float32)
    for group_index in range(N_DP):
        low_edge = group_index * group_rows
        partial_value = jnp.dot(left_side[low_edge:low_edge + group_rows].T, right_side[low_edge:low_edge + group_rows], preferred_element_type=jnp.float32)
        running = running + rounded(partial_value)
    return running

def reference(tokens, neighbour_buffer, shard_ids, row_ids, query_weight, key_weight, value_weight, output_weight, up_weight, down_weight, grad_output):
    head_group = HEADS * HD // N_TENSOR
    unit_group = FF // N_TENSOR
    score_factor = 1.0 / math.sqrt(HD)
    token_f = tokens.astype(jnp.float32)
    base_scale = rms_scale(token_f)
    normed = (token_f * base_scale).astype(jnp.bfloat16)
    flat_ids = (shard_ids * BUF + row_ids).reshape(BLOCKS * 2).astype(jnp.int32)
    neighbours = jnp.take(neighbour_buffer, flat_ids, axis=0).reshape(BLOCKS * 2 * NLEN, D)
    query = jnp.dot(normed, query_weight, preferred_element_type=jnp.float32).astype(jnp.bfloat16)
    keys = jnp.dot(neighbours, key_weight, preferred_element_type=jnp.float32).astype(jnp.bfloat16)
    values = jnp.dot(neighbours, value_weight, preferred_element_type=jnp.float32).astype(jnp.bfloat16)
    query_heads = query.reshape(BLOCKS, BLOCK, HEADS, HD).astype(jnp.float32)
    key_heads = keys.reshape(BLOCKS, 2 * NLEN, HEADS, HD).astype(jnp.float32)
    value_heads = values.reshape(BLOCKS, 2 * NLEN, HEADS, HD).astype(jnp.float32)
    scores = jnp.einsum('cqhd,ckhd->chqk', query_heads, key_heads) * score_factor
    raised = jnp.exp(scores)
    attention = raised / lax.optimization_barrier(jnp.sum(raised, axis=-1, keepdims=True))
    attention_b = attention.astype(jnp.bfloat16)
    head_mix = jnp.einsum('chqk,ckhd->cqhd', attention_b.astype(jnp.float32), value_heads).astype(jnp.bfloat16)
    mix_rows = head_mix.reshape(TOKENS, HEADS * HD)
    attn_out = split_sum(mix_rows, output_weight, head_group)
    resid_f = rounded(token_f + attn_out)
    resid_scale = rms_scale(resid_f)
    ffn_in = (resid_f * resid_scale).astype(jnp.bfloat16)
    pre_act = jnp.dot(ffn_in, up_weight, preferred_element_type=jnp.float32)
    activated = gelu_value(pre_act).astype(jnp.bfloat16)
    ffn_out = split_sum(activated, down_weight, unit_group)
    layer_out = (resid_f + ffn_out).astype(jnp.bfloat16)
    grad_act = jnp.dot(grad_output, down_weight.T, preferred_element_type=jnp.float32)
    grad_pre = (grad_act * gelu_slope(pre_act)).astype(jnp.bfloat16)
    grad_norm = split_sum(grad_pre, up_weight.T, unit_group)
    grad_resid = (grad_output.astype(jnp.float32) + norm_back(resid_f, resid_scale, grad_norm)).astype(jnp.bfloat16)
    grad_mix = jnp.dot(grad_resid, output_weight.T, preferred_element_type=jnp.float32).astype(jnp.bfloat16)
    mix_heads_grad = grad_mix.reshape(BLOCKS, BLOCK, HEADS, HD).astype(jnp.float32)
    grad_probs = jnp.einsum('cqhd,ckhd->chqk', mix_heads_grad, value_heads)
    row_dot = jnp.einsum('cqhd,cqhd->chq', mix_heads_grad, head_mix.astype(jnp.float32))[..., None]
    grad_scores = (attention * (grad_probs - row_dot) * score_factor).astype(jnp.bfloat16).astype(jnp.float32)
    grad_query = jnp.einsum('chqk,ckhd->cqhd', grad_scores, key_heads).astype(jnp.bfloat16).reshape(TOKENS, HEADS * HD)
    grad_keys = jnp.einsum('chqk,cqhd->ckhd', grad_scores, query_heads).astype(jnp.bfloat16).reshape(BLOCKS * 2 * NLEN, HEADS * HD)
    grad_values = jnp.einsum('chqk,cqhd->ckhd', attention_b.astype(jnp.float32), mix_heads_grad).astype(jnp.bfloat16).reshape(BLOCKS * 2 * NLEN, HEADS * HD)
    query_grad = group_grad(normed, grad_query, TOK_DEV)
    key_grad = group_grad(neighbours, grad_keys, BLK_DEV * 2 * NLEN)
    value_grad = group_grad(neighbours, grad_values, BLK_DEV * 2 * NLEN)
    mix_grad = group_grad(mix_rows, grad_resid, TOK_DEV)
    grad_in = split_sum(grad_query, query_weight.T, head_group)
    grad_tokens = (grad_resid.astype(jnp.float32) + norm_back(token_f, base_scale, grad_in)).astype(jnp.bfloat16)
    return (layer_out, grad_tokens, query_grad, key_grad, value_grad, mix_grad)
```

```python
import math

import jax
import jax.numpy as jnp
from jax import lax
from jax.sharding import PartitionSpec as P

HD = 128
BLOCK = 64
NLEN = 128
SIDE = 4


epsilon = 1e-06
gelu_root = 0.7978845608028654
gelu_cubic = 0.044715


def rms_scale(values):
    return lax.rsqrt(jnp.mean(values * values, axis=-1, keepdims=True) + epsilon)


def norm_back(values, factor, incoming):
    normal_part = values * factor
    return (
        incoming - normal_part * jnp.mean(incoming * normal_part, axis=-1, keepdims=True)
    ) * factor


def gelu_value(inputs):
    inner = gelu_root * (inputs + gelu_cubic * inputs * inputs * inputs)
    return 0.5 * inputs * (1.0 + jnp.tanh(inner))


def gelu_slope(inputs):
    inner = gelu_root * (inputs + gelu_cubic * inputs * inputs * inputs)
    tanh_part = jnp.tanh(inner)
    return 0.5 * (1.0 + tanh_part) + 0.5 * inputs * (1.0 - tanh_part * tanh_part) * gelu_root * (
        1.0 + 3.0 * gelu_cubic * inputs * inputs
    )


def rounded(partial_value):
    return lax.optimization_barrier(partial_value.astype(jnp.bfloat16)).astype(jnp.float32)


def contract_last(left_side, right_side):
    return lax.dot_general(
        left_side, right_side, (((1,), (1,)), ((), ())), preferred_element_type=jnp.float32
    )


def contract_first(left_side, right_side):
    return lax.dot_general(
        left_side, right_side, (((0,), (0,)), ((), ())), preferred_element_type=jnp.float32
    )


def plane_shift(along_x, step):
    pairs = []
    for place in range(SIDE * SIDE):
        y, x = divmod(place, SIDE)
        target = SIDE * y + (x + step) % SIDE if along_x else SIDE * ((y + step) % SIDE) + x
        pairs.append((place, target))
    return pairs


def ring_gather(piece, along_x, split_axis):
    place = lax.axis_index("tensor")
    here = place % SIDE if along_x else place // SIDE
    forward, backward = plane_shift(along_x, 1), plane_shift(along_x, -1)
    from_prev = lax.ppermute(piece, "tensor", forward)
    from_next = lax.ppermute(piece, "tensor", backward)
    half = piece.shape[split_axis] // 2
    first = lax.slice_in_dim(from_prev, 0, half, axis=split_axis)
    second = lax.slice_in_dim(from_next, half, 2 * half, axis=split_axis)
    opposite = jnp.concatenate(
        [lax.ppermute(first, "tensor", forward), lax.ppermute(second, "tensor", backward)],
        axis=split_axis,
    )
    stacked = jnp.zeros((SIDE,) + piece.shape, piece.dtype)
    for shift, part in ((0, piece), (-1, from_prev), (1, from_next), (2, opposite)):
        stacked = lax.dynamic_update_index_in_dim(stacked, part, (here + shift) % SIDE, 0)
    return stacked


def plane_gather(piece, halve_axis, split_axis):
    half = piece.shape[halve_axis] // 2
    first = lax.slice_in_dim(piece, 0, half, axis=halve_axis)
    second = lax.slice_in_dim(piece, half, 2 * half, axis=halve_axis)
    first = ring_gather(first, True, split_axis)
    second = ring_gather(second, False, split_axis)
    first = ring_gather(first, False, split_axis + 1)
    second = ring_gather(second, True, split_axis + 1)
    return first, jnp.swapaxes(second, 0, 1)


def gather_rows(rows):
    first, second = plane_gather(rows, 1, 1)
    count = SIDE * SIDE * rows.shape[0]
    half = rows.shape[1] // 2
    return jnp.concatenate([first.reshape(count, half), second.reshape(count, half)], axis=1)


def scatter_sum(partial_rows):
    size = lax.axis_size("tensor")
    share = partial_rows.shape[0] // size
    swapped = lax.all_to_all(
        partial_rows.astype(jnp.bfloat16).reshape(size, share, partial_rows.shape[1]),
        "tensor",
        split_axis=0,
        concat_axis=0,
        tiled=True,
    )
    return jnp.sum(swapped.astype(jnp.float32), axis=0)


def local(
    tokens,
    neighbour_buffer,
    shard_ids,
    row_ids,
    query_weight,
    key_weight,
    value_weight,
    output_weight,
    up_weight,
    down_weight,
    grad_output,
):
    data_size = lax.axis_size("dp")
    tensor_size = lax.axis_size("tensor")
    token_count = tokens.shape[0]
    width = tokens.shape[1]
    block_count = shard_ids.shape[0]
    capacity = block_count // 2
    pair_count = 2 * block_count
    owners = shard_ids.reshape(pair_count)
    wanted = row_ids.reshape(pair_count)
    same_owner = owners[:, None] == owners[None, :]
    earlier = lax.broadcasted_iota(jnp.int32, (pair_count, pair_count), 0) < lax.broadcasted_iota(
        jnp.int32, (pair_count, pair_count), 1
    )
    slot_index = jnp.sum((same_owner & earlier).astype(jnp.int32), axis=0)
    owner_grid = lax.broadcasted_iota(jnp.int32, (data_size, capacity, pair_count), 0)
    slot_grid = lax.broadcasted_iota(jnp.int32, (data_size, capacity, pair_count), 1)
    slot_match = (owners[None, None, :] == owner_grid) & (slot_index[None, None, :] == slot_grid)
    requests = jnp.sum(jnp.where(slot_match, wanted[None, None, :], 0), axis=2)
    replies = lax.all_to_all(
        jnp.take(
            neighbour_buffer,
            lax.all_to_all(requests, "dp", split_axis=0, concat_axis=0, tiled=True),
            axis=0,
        ),
        "dp",
        split_axis=0,
        concat_axis=0,
        tiled=True,
    )
    reply_rows = replies.reshape(data_size * capacity, replies.shape[2], replies.shape[3])
    local_enc = jnp.take(reply_rows, owners * capacity + slot_index, axis=0)
    local_enc, up_weight, down_weight = lax.optimization_barrier(
        (local_enc, up_weight, down_weight)
    )
    up_full, down_full = (
        lax.all_gather(up_weight, "dp", axis=0, tiled=True),
        lax.all_gather(down_weight, "dp", axis=1, tiled=True),
    )
    enc_a, enc_b = plane_gather(local_enc.reshape(pair_count * NLEN, width // tensor_size), 0, 0)
    half_rows = pair_count * NLEN // 2
    enc_rows = jnp.concatenate(
        [
            enc_a.transpose(2, 0, 1, 3).reshape(half_rows, width),
            enc_b.transpose(2, 0, 1, 3).reshape(half_rows, width),
        ],
        axis=0,
    )
    token_f = tokens.astype(jnp.float32)
    base_scale = rms_scale(token_f)
    normed = (token_f * base_scale).astype(jnp.bfloat16)
    query_rows = jnp.dot(normed, query_weight, preferred_element_type=jnp.float32).astype(
        jnp.bfloat16
    )
    head_width = query_rows.shape[1]
    both_weights = jnp.concatenate([key_weight, value_weight], axis=1)
    both_rows = jnp.dot(enc_rows, both_weights, preferred_element_type=jnp.float32).astype(
        jnp.bfloat16
    )
    key_rows = both_rows[:, :head_width]
    value_rows = both_rows[:, head_width:]
    heads_here = head_width // HD
    query_heads = query_rows.reshape(block_count, BLOCK, heads_here, HD)
    key_heads = key_rows.reshape(block_count, 2 * NLEN, heads_here, HD)
    value_heads = value_rows.reshape(block_count, 2 * NLEN, heads_here, HD)
    score_factor = 1.0 / math.sqrt(HD)
    scores = (
        jnp.einsum("cqhd,ckhd->chqk", query_heads, key_heads, preferred_element_type=jnp.float32)
        * score_factor
    )
    raised = jnp.exp(scores)
    attention = raised / jnp.sum(raised, axis=-1, keepdims=True)
    attention_b = attention.astype(jnp.bfloat16)
    head_mix = jnp.einsum(
        "chqk,ckhd->cqhd", attention_b, value_heads, preferred_element_type=jnp.float32
    ).astype(jnp.bfloat16)
    mix_rows = head_mix.reshape(token_count, head_width)
    attn_part = jnp.dot(mix_rows, output_weight, preferred_element_type=jnp.float32)
    rows_share = token_count // tensor_size
    row_start = lax.axis_index("tensor") * rows_share
    token_rows = lax.dynamic_slice_in_dim(token_f, row_start, rows_share, 0)
    base_rows = lax.dynamic_slice_in_dim(base_scale, row_start, rows_share, 0)
    attn_rows = scatter_sum(attn_part)
    resid_f = rounded(token_rows + attn_rows)
    resid_scale = rms_scale(resid_f)
    ffn_in = gather_rows((resid_f * resid_scale).astype(jnp.bfloat16))
    pre_act = jnp.dot(ffn_in, up_full, preferred_element_type=jnp.float32)
    activated = gelu_value(pre_act).astype(jnp.bfloat16)
    grad_act = contract_last(grad_output, down_full)
    grad_pre = (grad_act * gelu_slope(pre_act)).astype(jnp.bfloat16)
    norm_part = contract_last(grad_pre, up_full)
    norm_rows = scatter_sum(norm_part)
    out_rows = lax.dynamic_slice_in_dim(grad_output, row_start, rows_share, 0).astype(jnp.float32)
    grad_resid_rows = (out_rows + norm_back(resid_f, resid_scale, norm_rows)).astype(jnp.bfloat16)
    grad_resid = gather_rows(grad_resid_rows)
    grad_mix = contract_last(grad_resid, output_weight).astype(jnp.bfloat16)
    mix_heads_grad = grad_mix.reshape(block_count, BLOCK, heads_here, HD)
    grad_probs = jnp.einsum(
        "cqhd,ckhd->chqk", mix_heads_grad, value_heads, preferred_element_type=jnp.float32
    )
    row_dot = jnp.einsum(
        "cqhd,cqhd->chq", mix_heads_grad, head_mix, preferred_element_type=jnp.float32
    )[..., None]
    grad_scores = (attention * (grad_probs - row_dot) * score_factor).astype(jnp.bfloat16)
    grad_query = (
        jnp.einsum("chqk,ckhd->cqhd", grad_scores, key_heads, preferred_element_type=jnp.float32)
        .astype(jnp.bfloat16)
        .reshape(token_count, head_width)
    )
    grad_keys = (
        jnp.einsum("chqk,cqhd->ckhd", grad_scores, query_heads, preferred_element_type=jnp.float32)
        .astype(jnp.bfloat16)
        .reshape(pair_count * NLEN, head_width)
    )
    grad_values = (
        jnp.einsum(
            "chqk,cqhd->ckhd", attention_b, mix_heads_grad, preferred_element_type=jnp.float32
        )
        .astype(jnp.bfloat16)
        .reshape(pair_count * NLEN, head_width)
    )
    weight_parts = jnp.concatenate(
        [
            contract_first(normed, grad_query),
            contract_first(enc_rows, jnp.concatenate([grad_keys, grad_values], axis=1)),
            contract_first(grad_resid, mix_rows),
        ],
        axis=1,
    ).astype(jnp.bfloat16)
    summed = lax.psum_scatter(
        weight_parts, "dp", scatter_dimension=0, tiled=True
    ).astype(jnp.float32)
    query_grad = summed[:, :head_width]
    key_grad = summed[:, head_width : 2 * head_width]
    value_grad = summed[:, 2 * head_width : 3 * head_width]
    mix_grad = summed[:, 3 * head_width :].T
    activated, grad_query, _ = lax.optimization_barrier((activated, grad_query, weight_parts))
    ffn_part = jnp.dot(activated, down_full, preferred_element_type=jnp.float32)
    input_part = contract_last(grad_query, query_weight)
    layer_out = (resid_f + scatter_sum(ffn_part)).astype(jnp.bfloat16)
    input_rows = scatter_sum(input_part)
    grad_tokens = (
        grad_resid_rows.astype(jnp.float32) + norm_back(token_rows, base_rows, input_rows)
    ).astype(jnp.bfloat16)
    return (layer_out, grad_tokens, query_grad, key_grad, value_grad, mix_grad)


def solution(mesh):
    in_specs = (
        P("dp", None),
        P("dp", None, "tensor"),
        P("dp", None),
        P("dp", None),
        P(None, "tensor"),
        P(None, "tensor"),
        P(None, "tensor"),
        P("tensor", None),
        P("dp", "tensor"),
        P("tensor", "dp"),
        P("dp", None),
    )
    out_specs = (
        P(("dp", "tensor"), None),
        P(("dp", "tensor"), None),
        P("dp", "tensor"),
        P("dp", "tensor"),
        P("dp", "tensor"),
        P("tensor", "dp"),
    )
    return jax.shard_map(local, mesh=mesh, in_specs=in_specs, out_specs=out_specs, check_vma=False)
```

```python
import math

import jax
import jax.numpy as jnp
from jax import lax
from jax.sharding import PartitionSpec as P

HD = 128
BLOCK = 64
NLEN = 128
SIDE = 4


epsilon = 1e-06
gelu_root = 0.7978845608028654
gelu_cubic = 0.044715


def rms_scale(values):
    return lax.rsqrt(jnp.mean(values * values, axis=-1, keepdims=True) + epsilon)


def norm_back(values, factor, incoming):
    normal_part = values * factor
    return (
        incoming - normal_part * jnp.mean(incoming * normal_part, axis=-1, keepdims=True)
    ) * factor


def gelu_value(inputs):
    inner = gelu_root * (inputs + gelu_cubic * inputs * inputs * inputs)
    return 0.5 * inputs * (1.0 + jnp.tanh(inner))


def gelu_slope(inputs):
    inner = gelu_root * (inputs + gelu_cubic * inputs * inputs * inputs)
    tanh_part = jnp.tanh(inner)
    return 0.5 * (1.0 + tanh_part) + 0.5 * inputs * (1.0 - tanh_part * tanh_part) * gelu_root * (
        1.0 + 3.0 * gelu_cubic * inputs * inputs
    )


def rounded(partial_value):
    return lax.optimization_barrier(partial_value.astype(jnp.bfloat16)).astype(jnp.float32)


def contract_last(left_side, right_side):
    return lax.dot_general(
        left_side, right_side, (((1,), (1,)), ((), ())), preferred_element_type=jnp.float32
    )


def contract_first(left_side, right_side):
    return lax.dot_general(
        left_side, right_side, (((0,), (0,)), ((), ())), preferred_element_type=jnp.float32
    )


def plane_shift(along_x, step):
    pairs = []
    for place in range(SIDE * SIDE):
        y, x = divmod(place, SIDE)
        target = SIDE * y + (x + step) % SIDE if along_x else SIDE * ((y + step) % SIDE) + x
        pairs.append((place, target))
    return pairs


def ring_gather(piece, along_x, split_axis):
    place = lax.axis_index("tensor")
    here = lax.rem(place, SIDE) if along_x else lax.div(place, SIDE)
    forward, backward = plane_shift(along_x, 1), plane_shift(along_x, -1)
    from_prev = lax.ppermute(piece, "tensor", forward)
    from_next = lax.ppermute(piece, "tensor", backward)
    half = piece.shape[split_axis] // 2
    first = lax.slice_in_dim(from_prev, 0, half, axis=split_axis)
    second = lax.slice_in_dim(from_next, half, 2 * half, axis=split_axis)
    opposite = jnp.concatenate(
        [lax.ppermute(first, "tensor", forward), lax.ppermute(second, "tensor", backward)],
        axis=split_axis,
    )
    stacked = jnp.zeros((SIDE,) + piece.shape, piece.dtype)
    for shift, part in ((0, piece), (-1, from_prev), (1, from_next), (2, opposite)):
        stacked = lax.dynamic_update_index_in_dim(stacked, part, lax.rem(here + shift + SIDE, SIDE), 0)
    return stacked


def plane_gather(piece):
    feature_count, row_count = piece.shape
    half = feature_count // 2
    first = ring_gather(ring_gather(piece[:half], True, 0), False, 1)
    second = ring_gather(ring_gather(piece[half:], False, 0), True, 1)
    both = jnp.stack([first, jnp.swapaxes(second, 0, 1)], axis=2)
    return both.reshape(SIDE * SIDE * feature_count, row_count)


def gather_rows(rows):
    size = lax.axis_size("tensor")
    copies = jnp.broadcast_to(rows[None], (size,) + rows.shape)
    gathered = lax.all_to_all(copies, "tensor", split_axis=0, concat_axis=0, tiled=True)
    return gathered.reshape(size * rows.shape[0], rows.shape[1])


def scatter_sum(partial_rows):
    size = lax.axis_size("tensor")
    share = partial_rows.shape[0] // size
    swapped = lax.all_to_all(
        partial_rows.astype(jnp.bfloat16).reshape(size, share, partial_rows.shape[1]),
        "tensor",
        split_axis=0,
        concat_axis=0,
        tiled=True,
    )
    return jnp.sum(swapped.astype(jnp.float32), axis=0)


def data_sum(parts):
    size = lax.axis_size("dp")
    core = lax.axis_index("dp") % 2

    def shares_of(parity):
        shares = [part.reshape(size // 2, 2, -1, part.shape[1]) for part in parts]
        return jnp.stack(
            [lax.dynamic_index_in_dim(share, parity, 1, keepdims=False) for share in shares], axis=1
        ).astype(jnp.bfloat16)

    got = lax.ppermute(
        shares_of(1 - core), "dp", [(place, place ^ 1) for place in range(size)]
    )
    paired = (shares_of(core).astype(jnp.float32) + got.astype(jnp.float32)).astype(jnp.bfloat16)
    groups = [list(range(parity, size, 2)) for parity in range(2)]
    return lax.psum_scatter(
        paired, "dp", scatter_dimension=0, axis_index_groups=groups, tiled=False
    )


def local(
    tokens,
    neighbour_buffer,
    shard_ids,
    row_ids,
    query_weight,
    key_weight,
    value_weight,
    output_weight,
    up_weight,
    down_weight,
    grad_output,
):
    data_size = lax.axis_size("dp")
    tensor_size = lax.axis_size("tensor")
    token_count = tokens.shape[0]
    width = tokens.shape[1]
    block_count = shard_ids.shape[0]
    capacity = block_count // 2
    pair_count = 2 * block_count
    owners = shard_ids.reshape(pair_count)
    wanted = row_ids.reshape(pair_count)
    same_owner = owners[:, None] == owners[None, :]
    earlier = lax.broadcasted_iota(jnp.int32, (pair_count, pair_count), 0) < lax.broadcasted_iota(
        jnp.int32, (pair_count, pair_count), 1
    )
    slot_index = jnp.sum((same_owner & earlier).astype(jnp.int32), axis=0)
    owner_grid = lax.broadcasted_iota(jnp.int32, (data_size, capacity, pair_count), 0)
    slot_grid = lax.broadcasted_iota(jnp.int32, (data_size, capacity, pair_count), 1)
    slot_match = (owners[None, None, :] == owner_grid) & (slot_index[None, None, :] == slot_grid)
    requests = jnp.sum(jnp.where(slot_match, wanted[None, None, :], 0), axis=2)
    asked = lax.all_to_all(requests, "dp", split_axis=0, concat_axis=0, tiled=True)
    half_len = NLEN // 2
    buffer_halves = neighbour_buffer.reshape(-1, half_len, neighbour_buffer.shape[2])

    def fetch(part, after=None):
        sent = jnp.take(buffer_halves, 2 * asked + part, axis=0, mode="clip")
        if after is not None:
            sent, after = lax.optimization_barrier((sent, after))
        replies = lax.all_to_all(sent, "dp", split_axis=0, concat_axis=0, tiled=True)
        reply_rows = replies.reshape((data_size * capacity,) + replies.shape[2:])
        mine = jnp.take(reply_rows, owners * capacity + slot_index, axis=0, mode="clip")
        return mine.reshape(pair_count * half_len, -1).T, after

    enc_mine, _ = fetch(0)
    enc_other, enc_mine = fetch(1, enc_mine)
    enc_first = lax.all_gather(enc_mine, "tensor", axis=0, tiled=True)
    enc_other, up_weight, down_weight = lax.optimization_barrier(
        (enc_other, up_weight, down_weight)
    )
    enc_second = plane_gather(enc_other)
    up_full, down_full = (
        lax.all_gather(up_weight, "dp", axis=0, tiled=True),
        lax.all_gather(down_weight, "dp", axis=1, tiled=True),
    )
    token_f = tokens.astype(jnp.float32)
    base_scale = rms_scale(token_f)
    normed = (token_f * base_scale).astype(jnp.bfloat16)
    query_rows = jnp.dot(normed, query_weight, preferred_element_type=jnp.float32).astype(
        jnp.bfloat16
    )
    head_width = query_rows.shape[1]
    both_weights = jnp.concatenate([key_weight, value_weight], axis=1)
    both_heads = jnp.concatenate(
        [
            contract_first(part, both_weights)
            .astype(jnp.bfloat16)
            .reshape(block_count, NLEN, 2 * head_width)
            for part in (enc_first, enc_second)
        ],
        axis=1,
    )
    heads_here = head_width // HD
    query_heads = query_rows.reshape(block_count, BLOCK, heads_here, HD)
    key_heads = both_heads[:, :, :head_width].reshape(block_count, 2 * NLEN, heads_here, HD)
    value_heads = both_heads[:, :, head_width:].reshape(block_count, 2 * NLEN, heads_here, HD)
    score_factor = 1.0 / math.sqrt(HD)
    scores = (
        jnp.einsum("cqhd,ckhd->chqk", query_heads, key_heads, preferred_element_type=jnp.float32)
        * score_factor
    )
    raised = jnp.exp(scores)
    attention = raised / jnp.sum(raised, axis=-1, keepdims=True)
    attention_b = attention.astype(jnp.bfloat16)
    head_mix = jnp.einsum(
        "chqk,ckhd->cqhd", attention_b, value_heads, preferred_element_type=jnp.float32
    ).astype(jnp.bfloat16)
    mix_rows = head_mix.reshape(token_count, head_width)
    attn_part = jnp.dot(mix_rows, output_weight, preferred_element_type=jnp.float32)
    rows_share = token_count // tensor_size
    row_start = lax.axis_index("tensor") * rows_share
    token_rows = lax.dynamic_slice_in_dim(token_f, row_start, rows_share, 0)
    base_rows = lax.dynamic_slice_in_dim(base_scale, row_start, rows_share, 0)
    attn_rows = scatter_sum(attn_part)
    resid_f = rounded(token_rows + attn_rows)
    resid_scale = rms_scale(resid_f)
    ffn_in = gather_rows((resid_f * resid_scale).astype(jnp.bfloat16))
    pre_act = jnp.dot(ffn_in, up_full, preferred_element_type=jnp.float32)
    activated = gelu_value(pre_act).astype(jnp.bfloat16)
    grad_act = contract_last(grad_output, down_full)
    grad_pre = (grad_act * gelu_slope(pre_act)).astype(jnp.bfloat16)
    norm_part = contract_last(grad_pre, up_full)
    ffn_part = jnp.dot(activated, down_full, preferred_element_type=jnp.float32).astype(
        jnp.bfloat16
    )
    norm_rows, ffn_part = lax.optimization_barrier((scatter_sum(norm_part), ffn_part))
    ffn_rows_sum = lax.psum_scatter(ffn_part, "tensor", scatter_dimension=0, tiled=True)
    out_rows = lax.dynamic_slice_in_dim(grad_output, row_start, rows_share, 0).astype(jnp.float32)
    grad_resid_rows = (out_rows + norm_back(resid_f, resid_scale, norm_rows)).astype(jnp.bfloat16)
    grad_resid = gather_rows(grad_resid_rows)
    grad_mix = contract_last(grad_resid, output_weight).astype(jnp.bfloat16)
    mix_heads_grad = grad_mix.reshape(block_count, BLOCK, heads_here, HD)
    grad_probs = jnp.einsum(
        "cqhd,ckhd->chqk", mix_heads_grad, value_heads, preferred_element_type=jnp.float32
    )
    row_dot = jnp.einsum(
        "cqhd,cqhd->chq", mix_heads_grad, head_mix, preferred_element_type=jnp.float32
    )[..., None]
    grad_scores = (attention * (grad_probs - row_dot) * score_factor).astype(jnp.bfloat16)
    grad_query = (
        jnp.einsum("chqk,ckhd->cqhd", grad_scores, key_heads, preferred_element_type=jnp.float32)
        .astype(jnp.bfloat16)
        .reshape(token_count, head_width)
    )
    grad_keys = jnp.einsum(
        "chqk,cqhd->ckhd", grad_scores, query_heads, preferred_element_type=jnp.float32
    ).astype(jnp.bfloat16)
    grad_values = jnp.einsum(
        "chqk,cqhd->ckhd", attention_b, mix_heads_grad, preferred_element_type=jnp.float32
    ).astype(jnp.bfloat16)
    both_grads = jnp.concatenate([grad_keys, grad_values], axis=3).reshape(
        block_count, 2 * NLEN, 2 * head_width
    )
    enc_grad = jnp.dot(
        enc_first,
        both_grads[:, :NLEN].reshape(block_count * NLEN, 2 * head_width),
        preferred_element_type=jnp.float32,
    ) + jnp.dot(
        enc_second,
        both_grads[:, NLEN:].reshape(block_count * NLEN, 2 * head_width),
        preferred_element_type=jnp.float32,
    )
    enc_grad = enc_grad.astype(jnp.bfloat16)
    summed = data_sum(
        [
            contract_first(normed, grad_query).astype(jnp.bfloat16),
            enc_grad[:, :head_width],
            enc_grad[:, head_width:],
            contract_first(grad_resid, mix_rows).astype(jnp.bfloat16),
        ]
    ).astype(jnp.float32)
    query_grad, key_grad, value_grad = summed[0], summed[1], summed[2]
    mix_grad = summed[3].T
    input_part = contract_last(grad_query, query_weight)
    input_rows, ffn_rows_sum = lax.optimization_barrier((scatter_sum(input_part), ffn_rows_sum))
    layer_out = (resid_f + ffn_rows_sum.astype(jnp.float32)).astype(jnp.bfloat16)
    grad_tokens = (
        grad_resid_rows.astype(jnp.float32) + norm_back(token_rows, base_rows, input_rows)
    ).astype(jnp.bfloat16)
    return (layer_out, grad_tokens, query_grad, key_grad, value_grad, mix_grad)


def solution(mesh):
    in_specs = (
        P("dp", None),
        P("dp", None, "tensor"),
        P("dp", None),
        P("dp", None),
        P(None, "tensor"),
        P(None, "tensor"),
        P(None, "tensor"),
        P("tensor", None),
        P("dp", "tensor"),
        P("tensor", "dp"),
        P("dp", None),
    )
    out_specs = (
        P(("dp", "tensor"), None),
        P(("dp", "tensor"), None),
        P("dp", "tensor"),
        P("dp", "tensor"),
        P("dp", "tensor"),
        P("tensor", "dp"),
    )
    return jax.shard_map(local, mesh=mesh, in_specs=in_specs, out_specs=out_specs, check_vma=False)
```

```python
import math

import jax
import jax.numpy as jnp
from jax import lax
from jax.sharding import PartitionSpec as P

HD = 128
BLOCK = 64
NLEN = 128
GRAIN = 16
FIRST = 80


epsilon = 1e-06
gelu_root = 0.7978845608028654
gelu_cubic = 0.044715


def rms_scale(values):
    return lax.rsqrt(jnp.mean(values * values, axis=-1, keepdims=True) + epsilon)


def norm_back(values, factor, incoming):
    normal_part = values * factor
    return (
        incoming - normal_part * jnp.mean(incoming * normal_part, axis=-1, keepdims=True)
    ) * factor


def gelu_value(inputs):
    inner = gelu_root * (inputs + gelu_cubic * inputs * inputs * inputs)
    return 0.5 * inputs * (1.0 + jnp.tanh(inner))


def gelu_slope(inputs):
    inner = gelu_root * (inputs + gelu_cubic * inputs * inputs * inputs)
    tanh_part = jnp.tanh(inner)
    return 0.5 * (1.0 + tanh_part) + 0.5 * inputs * (1.0 - tanh_part * tanh_part) * gelu_root * (
        1.0 + 3.0 * gelu_cubic * inputs * inputs
    )


def rounded(partial_value):
    return lax.optimization_barrier(partial_value.astype(jnp.bfloat16)).astype(jnp.float32)


def contract_last(left_side, right_side):
    return lax.dot_general(
        left_side, right_side, (((1,), (1,)), ((), ())), preferred_element_type=jnp.float32
    )


def contract_first(left_side, right_side):
    return lax.dot_general(
        left_side, right_side, (((0,), (0,)), ((), ())), preferred_element_type=jnp.float32
    )


def gather_rows(rows):
    size = lax.axis_size("tensor")
    copies = jnp.broadcast_to(rows[None], (size,) + rows.shape)
    gathered = lax.all_to_all(copies, "tensor", split_axis=0, concat_axis=0, tiled=True)
    return gathered.reshape(size * rows.shape[0], rows.shape[1])


def swap_rows(partial_rows):
    size = lax.axis_size("tensor")
    share = partial_rows.shape[0] // size
    return lax.all_to_all(
        partial_rows.astype(jnp.bfloat16).reshape(size, share, partial_rows.shape[1]),
        "tensor",
        split_axis=0,
        concat_axis=0,
        tiled=True,
    )


def add_up(swapped):
    return jnp.sum(swapped.astype(jnp.float32), axis=0)


def scatter_sum(partial_rows):
    return add_up(swap_rows(partial_rows))


def data_sum(parts, after):
    size = lax.axis_size("dp")
    core = lax.axis_index("dp") % 2

    def shares_of(parity):
        shares = [part.reshape(size // 2, 2, -1, part.shape[1]) for part in parts]
        return jnp.stack(
            [lax.dynamic_index_in_dim(share, parity, 1, keepdims=False) for share in shares], axis=1
        ).astype(jnp.bfloat16)

    got = lax.ppermute(
        shares_of(1 - core), "dp", [(place, place ^ 1) for place in range(size)]
    )
    paired = (shares_of(core).astype(jnp.float32) + got.astype(jnp.float32)).astype(jnp.bfloat16)
    paired, after = lax.optimization_barrier((paired, after))
    groups = [list(range(parity, size, 2)) for parity in range(2)]
    summed = lax.psum_scatter(
        paired, "dp", scatter_dimension=0, axis_index_groups=groups, tiled=False
    )
    return summed, after


def local(
    tokens,
    neighbour_buffer,
    shard_ids,
    row_ids,
    query_weight,
    key_weight,
    value_weight,
    output_weight,
    up_weight,
    down_weight,
    grad_output,
):
    data_size = lax.axis_size("dp")
    tensor_size = lax.axis_size("tensor")
    token_count = tokens.shape[0]
    width = tokens.shape[1]
    block_count = shard_ids.shape[0]
    capacity = block_count // 2
    pair_count = 2 * block_count
    owners = shard_ids.reshape(pair_count)
    wanted = row_ids.reshape(pair_count)
    same_owner = owners[:, None] == owners[None, :]
    earlier = lax.broadcasted_iota(jnp.int32, (pair_count, pair_count), 0) < lax.broadcasted_iota(
        jnp.int32, (pair_count, pair_count), 1
    )
    slot_index = jnp.sum((same_owner & earlier).astype(jnp.int32), axis=0)
    owner_grid = lax.broadcasted_iota(jnp.int32, (data_size, capacity, pair_count), 0)
    slot_grid = lax.broadcasted_iota(jnp.int32, (data_size, capacity, pair_count), 1)
    slot_match = (owners[None, None, :] == owner_grid) & (slot_index[None, None, :] == slot_grid)
    requests = jnp.sum(jnp.where(slot_match, wanted[None, None, :], 0), axis=2)
    asked = lax.all_to_all(requests, "dp", split_axis=0, concat_axis=0, tiled=True)
    grains = NLEN // GRAIN
    buffer_grains = neighbour_buffer.reshape(-1, GRAIN, neighbour_buffer.shape[2])

    def fetch(low, high, after=None):
        places = asked[..., None] * grains + jnp.arange(low // GRAIN, high // GRAIN)
        sent = jnp.take(buffer_grains, places, axis=0, mode="clip").reshape(
            asked.shape[:2] + (high - low, -1)
        )
        if after is not None:
            sent, after = lax.optimization_barrier((sent, after))
        replies = lax.all_to_all(sent, "dp", split_axis=0, concat_axis=0, tiled=True)
        reply_rows = replies.reshape((data_size * capacity,) + replies.shape[2:])
        mine = jnp.take(reply_rows, owners * capacity + slot_index, axis=0, mode="clip")
        return mine.reshape(pair_count * (high - low), -1).T, after

    enc_mine, _ = fetch(0, FIRST)
    enc_other, enc_mine = fetch(FIRST, NLEN, enc_mine)
    enc_first = lax.all_gather(enc_mine, "tensor", axis=0, tiled=True)
    frozen = jnp.concatenate([up_weight, down_weight.T], axis=1)
    enc_other, frozen = lax.optimization_barrier((enc_other, frozen))
    enc_second = gather_rows(enc_other)
    frozen_full = lax.all_gather(frozen, "dp", axis=0, tiled=True)
    hidden = up_weight.shape[1]
    up_full = frozen_full[:, :hidden]
    down_turned = frozen_full[:, hidden:]
    token_f = tokens.astype(jnp.float32)
    base_scale = rms_scale(token_f)
    normed = (token_f * base_scale).astype(jnp.bfloat16)
    query_rows = jnp.dot(normed, query_weight, preferred_element_type=jnp.float32).astype(
        jnp.bfloat16
    )
    head_width = query_rows.shape[1]
    both_weights = jnp.concatenate([key_weight, value_weight], axis=1)
    both_heads = jnp.concatenate(
        [
            contract_first(part, both_weights)
            .astype(jnp.bfloat16)
            .reshape(block_count, -1, 2 * head_width)
            for part in (enc_first, enc_second)
        ],
        axis=1,
    )
    heads_here = head_width // HD
    query_heads = query_rows.reshape(block_count, BLOCK, heads_here, HD)
    key_heads = both_heads[:, :, :head_width].reshape(block_count, 2 * NLEN, heads_here, HD)
    value_heads = both_heads[:, :, head_width:].reshape(block_count, 2 * NLEN, heads_here, HD)
    score_factor = 1.0 / math.sqrt(HD)
    scores = (
        jnp.einsum("cqhd,ckhd->chqk", query_heads, key_heads, preferred_element_type=jnp.float32)
        * score_factor
    )
    raised = jnp.exp(scores)
    attention = raised / jnp.sum(raised, axis=-1, keepdims=True)
    attention_b = attention.astype(jnp.bfloat16)
    head_mix = jnp.einsum(
        "chqk,ckhd->cqhd", attention_b, value_heads, preferred_element_type=jnp.float32
    ).astype(jnp.bfloat16)
    mix_rows = head_mix.reshape(token_count, head_width)
    attn_part = jnp.dot(mix_rows, output_weight, preferred_element_type=jnp.float32)
    rows_share = token_count // tensor_size
    row_start = lax.axis_index("tensor") * rows_share
    token_rows = lax.dynamic_slice_in_dim(token_f, row_start, rows_share, 0)
    base_rows = lax.dynamic_slice_in_dim(base_scale, row_start, rows_share, 0)
    attn_rows = scatter_sum(attn_part)
    resid_f = rounded(token_rows + attn_rows)
    resid_scale = rms_scale(resid_f)
    ffn_in = gather_rows((resid_f * resid_scale).astype(jnp.bfloat16))
    grad_act = lax.optimization_barrier(
        jnp.dot(grad_output, down_turned, preferred_element_type=jnp.float32)
    )
    pre_act = jnp.dot(ffn_in, up_full, preferred_element_type=jnp.float32)
    activated = gelu_value(pre_act).astype(jnp.bfloat16)
    grad_pre = (grad_act * gelu_slope(pre_act)).astype(jnp.bfloat16)
    norm_part = contract_last(grad_pre, up_full)
    ffn_part = contract_last(activated, down_turned).astype(jnp.bfloat16)
    norm_rows = scatter_sum(norm_part)
    out_rows = lax.dynamic_slice_in_dim(grad_output, row_start, rows_share, 0).astype(jnp.float32)
    grad_resid_rows = (out_rows + norm_back(resid_f, resid_scale, norm_rows)).astype(jnp.bfloat16)
    grad_resid, ffn_part = lax.optimization_barrier((gather_rows(grad_resid_rows), ffn_part))
    ffn_swapped = swap_rows(ffn_part)
    grad_mix = contract_last(grad_resid, output_weight).astype(jnp.bfloat16)
    mix_heads_grad = grad_mix.reshape(block_count, BLOCK, heads_here, HD)
    grad_probs = jnp.einsum(
        "cqhd,ckhd->chqk", mix_heads_grad, value_heads, preferred_element_type=jnp.float32
    )
    row_dot = jnp.einsum(
        "cqhd,cqhd->chq", mix_heads_grad, head_mix, preferred_element_type=jnp.float32
    )[..., None]
    grad_scores = (attention * (grad_probs - row_dot) * score_factor).astype(jnp.bfloat16)
    grad_query = (
        jnp.einsum("chqk,ckhd->cqhd", grad_scores, key_heads, preferred_element_type=jnp.float32)
        .astype(jnp.bfloat16)
        .reshape(token_count, head_width)
    )
    grad_keys = jnp.einsum(
        "chqk,cqhd->ckhd", grad_scores, query_heads, preferred_element_type=jnp.float32
    ).astype(jnp.bfloat16)
    grad_values = jnp.einsum(
        "chqk,cqhd->ckhd", attention_b, mix_heads_grad, preferred_element_type=jnp.float32
    ).astype(jnp.bfloat16)
    both_grads = jnp.concatenate([grad_keys, grad_values], axis=3).reshape(
        block_count, 2 * NLEN, 2 * head_width
    )
    enc_grad = jnp.dot(
        enc_first,
        both_grads[:, : 2 * FIRST].reshape(-1, 2 * head_width),
        preferred_element_type=jnp.float32,
    ) + jnp.dot(
        enc_second,
        both_grads[:, 2 * FIRST :].reshape(-1, 2 * head_width),
        preferred_element_type=jnp.float32,
    )
    enc_grad = enc_grad.astype(jnp.bfloat16)
    summed, grad_query = data_sum(
        [
            contract_first(normed, grad_query).astype(jnp.bfloat16),
            enc_grad[:, :head_width],
            enc_grad[:, head_width:],
            contract_first(grad_resid, mix_rows).astype(jnp.bfloat16),
        ],
        grad_query,
    )
    summed = summed.astype(jnp.float32)
    query_grad, key_grad, value_grad = summed[0], summed[1], summed[2]
    mix_grad = summed[3].T
    input_part = contract_last(grad_query, query_weight)
    input_rows = scatter_sum(input_part)
    layer_out = (resid_f + add_up(ffn_swapped)).astype(jnp.bfloat16)
    grad_tokens = (
        grad_resid_rows.astype(jnp.float32) + norm_back(token_rows, base_rows, input_rows)
    ).astype(jnp.bfloat16)
    return (layer_out, grad_tokens, query_grad, key_grad, value_grad, mix_grad)


def solution(mesh):
    in_specs = (
        P("dp", None),
        P("dp", None, "tensor"),
        P("dp", None),
        P("dp", None),
        P(None, "tensor"),
        P(None, "tensor"),
        P(None, "tensor"),
        P("tensor", None),
        P("dp", "tensor"),
        P("tensor", "dp"),
        P("dp", None),
    )
    out_specs = (
        P(("dp", "tensor"), None),
        P(("dp", "tensor"), None),
        P("dp", "tensor"),
        P("dp", "tensor"),
        P("dp", "tensor"),
        P("tensor", "dp"),
    )
    return jax.shard_map(local, mesh=mesh, in_specs=in_specs, out_specs=out_specs, check_vma=False)
```

```python
import math

import jax
import jax.numpy as jnp
from jax import lax
from jax.sharding import PartitionSpec as P

HD = 128
BLOCK = 64
NLEN = 128
SIDE = 4
ORDER = (0, -1, 1, 2)
PART = 64


epsilon = 1e-06
gelu_root = 0.7978845608028654
gelu_cubic = 0.044715


def rms_scale(values):
    return lax.rsqrt(jnp.mean(values * values, axis=-1, keepdims=True) + epsilon)


def norm_back(values, factor, incoming):
    normal_part = values * factor
    return (
        incoming - normal_part * jnp.mean(incoming * normal_part, axis=-1, keepdims=True)
    ) * factor


def gelu_value(inputs):
    inner = gelu_root * (inputs + gelu_cubic * inputs * inputs * inputs)
    return 0.5 * inputs * (1.0 + jnp.tanh(inner))


def gelu_slope(inputs):
    inner = gelu_root * (inputs + gelu_cubic * inputs * inputs * inputs)
    tanh_part = jnp.tanh(inner)
    return 0.5 * (1.0 + tanh_part) + 0.5 * inputs * (1.0 - tanh_part * tanh_part) * gelu_root * (
        1.0 + 3.0 * gelu_cubic * inputs * inputs
    )


def rounded(partial_value):
    return lax.optimization_barrier(partial_value.astype(jnp.bfloat16)).astype(jnp.float32)


def contract_last(left_side, right_side):
    return lax.dot_general(
        left_side, right_side, (((1,), (1,)), ((), ())), preferred_element_type=jnp.float32
    )


def contract_first(left_side, right_side):
    return lax.dot_general(
        left_side, right_side, (((0,), (0,)), ((), ())), preferred_element_type=jnp.float32
    )


def plane_shift(along_x, step):
    pairs = []
    for place in range(SIDE * SIDE):
        y, x = divmod(place, SIDE)
        target = SIDE * y + (x + step) % SIDE if along_x else SIDE * ((y + step) % SIDE) + x
        pairs.append((place, target))
    return pairs


def ring_parts(piece, along_x):
    forward, backward = plane_shift(along_x, 1), plane_shift(along_x, -1)
    before = lax.ppermute(piece, "tensor", forward)
    behind = lax.ppermute(piece, "tensor", backward)
    half = piece.shape[0] // 2
    opposite = jnp.concatenate(
        [
            lax.ppermute(before[:half], "tensor", forward),
            lax.ppermute(behind[half:], "tensor", backward),
        ],
        axis=0,
    )
    return [piece, before, behind, opposite]


def ring_sum_start(shares, along_x):
    place = lax.axis_index("tensor")
    here = lax.rem(place, SIDE) if along_x else lax.div(place, SIDE)
    mine, behind, ahead, opposite = [
        lax.dynamic_index_in_dim(shares, lax.rem(here + step + SIDE, SIDE), 0, keepdims=False)
        for step in ORDER
    ]
    half = opposite.shape[0] // 2
    first = lax.ppermute(opposite[:half], "tensor", plane_shift(along_x, 1))
    second = lax.ppermute(opposite[half:], "tensor", plane_shift(along_x, -1))
    ahead = jnp.concatenate([added(ahead[:half], first), ahead[half:]], axis=0)
    behind = jnp.concatenate([behind[:half], added(behind[half:], second)], axis=0)
    return mine, behind, ahead


def ring_sum_finish(parts, along_x):
    mine, behind, ahead = parts
    return added(
        mine,
        lax.ppermute(ahead, "tensor", plane_shift(along_x, 1)),
        lax.ppermute(behind, "tensor", plane_shift(along_x, -1)),
    )


def added(*terms):
    return sum(term.astype(jnp.float32) for term in terms).astype(jnp.bfloat16)


def plane_parts(piece):
    half = piece.shape[0] // 2
    first = jnp.concatenate(ring_parts(piece[:half], True), axis=0)
    second = jnp.concatenate(ring_parts(piece[half:], False), axis=0)
    return ring_parts(first, False) + ring_parts(second, True)


def bundle_blocks():
    place = lax.axis_index("tensor")
    steps = jnp.array(ORDER, jnp.int32) + SIDE
    rows = lax.rem(lax.div(place, SIDE) + steps, SIDE)
    columns = lax.rem(lax.rem(place, SIDE) + steps, SIDE)
    blocks = SIDE * rows[:, None] + columns[None, :]
    return jnp.concatenate([2 * blocks, 2 * blocks.T + 1], axis=0)


def gather_rows(rows):
    size = lax.axis_size("tensor")
    copies = jnp.broadcast_to(rows[None], (size,) + rows.shape)
    gathered = lax.all_to_all(copies, "tensor", split_axis=0, concat_axis=0, tiled=True)
    return gathered.reshape(size * rows.shape[0], rows.shape[1])


def scatter_sum(partial_rows):
    size = lax.axis_size("tensor")
    share = partial_rows.shape[0] // size
    swapped = lax.all_to_all(
        partial_rows.astype(jnp.bfloat16).reshape(size, share, partial_rows.shape[1]),
        "tensor",
        split_axis=0,
        concat_axis=0,
        tiled=True,
    )
    return jnp.sum(swapped.astype(jnp.float32), axis=0)


def data_sum(shares_of, after):
    size = lax.axis_size("dp")
    core = lax.axis_index("dp") % 2
    got = lax.ppermute(
        shares_of(1 - core), "dp", [(place, place ^ 1) for place in range(size)]
    )
    paired = (shares_of(core).astype(jnp.float32) + got.astype(jnp.float32)).astype(jnp.bfloat16)
    paired, after = lax.optimization_barrier((paired, after))
    groups = [list(range(parity, size, 2)) for parity in range(2)]
    summed = lax.psum_scatter(
        paired.reshape(-1, paired.shape[3]),
        "dp",
        scatter_dimension=0,
        axis_index_groups=groups,
        tiled=True,
    )
    return summed.reshape(paired.shape[1:]), after


def local(
    tokens,
    neighbour_buffer,
    shard_ids,
    row_ids,
    query_weight,
    key_weight,
    value_weight,
    output_weight,
    up_weight,
    down_weight,
    grad_output,
):
    data_size = lax.axis_size("dp")
    tensor_size = lax.axis_size("tensor")
    token_count = tokens.shape[0]
    width = tokens.shape[1]
    block_count = shard_ids.shape[0]
    capacity = block_count // 2
    pair_count = 2 * block_count
    owners = shard_ids.reshape(pair_count)
    wanted = row_ids.reshape(pair_count)
    same_owner = owners[:, None] == owners[None, :]
    earlier = lax.broadcasted_iota(jnp.int32, (pair_count, pair_count), 0) < lax.broadcasted_iota(
        jnp.int32, (pair_count, pair_count), 1
    )
    slot_index = jnp.sum((same_owner & earlier).astype(jnp.int32), axis=0)
    owner_grid = lax.broadcasted_iota(jnp.int32, (data_size, capacity, pair_count), 0)
    slot_grid = lax.broadcasted_iota(jnp.int32, (data_size, capacity, pair_count), 1)
    slot_match = (owners[None, None, :] == owner_grid) & (slot_index[None, None, :] == slot_grid)
    requests = jnp.sum(jnp.where(slot_match, wanted[None, None, :], 0), axis=2)
    asked = lax.all_to_all(requests, "dp", split_axis=0, concat_axis=0, tiled=True)
    buffer_parts = neighbour_buffer.reshape(-1, PART, neighbour_buffer.shape[2])
    part_count = NLEN // PART

    def fetch(part):
        sent = jnp.take(buffer_parts, asked * part_count + part, axis=0, mode="clip")
        replies = lax.all_to_all(sent, "dp", split_axis=0, concat_axis=0, tiled=True)
        reply_rows = replies.reshape((data_size * capacity,) + replies.shape[2:])
        mine = jnp.take(reply_rows, owners * capacity + slot_index, axis=0, mode="clip")
        return mine.reshape(pair_count * PART, -1).T

    enc_parts = []
    for part in range(part_count):
        enc_mine = fetch(part)
        if enc_parts:
            enc_mine, enc_parts[-1] = lax.optimization_barrier((enc_mine, enc_parts[-1]))
        enc_parts.append(plane_parts(enc_mine))
    frozen = jnp.concatenate([up_weight, down_weight.T], axis=1)
    enc_mine, frozen = lax.optimization_barrier((enc_mine, frozen))
    frozen_full = lax.all_gather(frozen, "dp", axis=0, tiled=True)
    hidden = up_weight.shape[1]
    up_full = frozen_full[:, :hidden]
    down_turned = frozen_full[:, hidden:]
    token_f = tokens.astype(jnp.float32)
    base_scale = rms_scale(token_f)
    normed = (token_f * base_scale).astype(jnp.bfloat16)
    query_rows = jnp.dot(normed, query_weight, preferred_element_type=jnp.float32).astype(
        jnp.bfloat16
    )
    head_width = query_rows.shape[1]
    both_weights = jnp.concatenate([key_weight, value_weight], axis=1)
    blocks = bundle_blocks()
    half_block = width // (2 * SIDE * SIDE)
    bundle_weights = jnp.take(
        both_weights.reshape(-1, half_block, 2 * head_width), blocks, axis=0, mode="clip"
    ).reshape(2 * SIDE, SIDE * half_block, 2 * head_width)
    both_heads = jnp.concatenate(
        [
            sum(contract_first(bundle, bundle_weights[at]) for at, bundle in enumerate(bundles))
            .astype(jnp.bfloat16)
            .reshape(block_count, 2 * PART, 2 * head_width)
            for bundles in enc_parts
        ],
        axis=1,
    )
    heads_here = head_width // HD
    query_heads = query_rows.reshape(block_count, BLOCK, heads_here, HD)
    key_heads = both_heads[:, :, :head_width].reshape(block_count, 2 * NLEN, heads_here, HD)
    value_heads = both_heads[:, :, head_width:].reshape(block_count, 2 * NLEN, heads_here, HD)
    score_factor = 1.0 / math.sqrt(HD)
    scores = (
        jnp.einsum("cqhd,ckhd->chqk", query_heads, key_heads, preferred_element_type=jnp.float32)
        * score_factor
    )
    raised = jnp.exp(scores)
    attention = raised / jnp.sum(raised, axis=-1, keepdims=True)
    attention_b = attention.astype(jnp.bfloat16)
    head_mix = jnp.einsum(
        "chqk,ckhd->cqhd", attention_b, value_heads, preferred_element_type=jnp.float32
    ).astype(jnp.bfloat16)
    mix_rows = head_mix.reshape(token_count, head_width)
    attn_part = jnp.dot(mix_rows, output_weight, preferred_element_type=jnp.float32)
    rows_share = token_count // tensor_size
    row_start = lax.axis_index("tensor") * rows_share
    token_rows = lax.dynamic_slice_in_dim(token_f, row_start, rows_share, 0)
    base_rows = lax.dynamic_slice_in_dim(base_scale, row_start, rows_share, 0)
    attn_rows = scatter_sum(attn_part)
    resid_f = rounded(token_rows + attn_rows)
    resid_scale = rms_scale(resid_f)
    ffn_in = gather_rows((resid_f * resid_scale).astype(jnp.bfloat16))
    grad_act = lax.optimization_barrier(
        jnp.dot(grad_output, down_turned, preferred_element_type=jnp.float32)
    )
    pre_act = jnp.dot(ffn_in, up_full, preferred_element_type=jnp.float32)
    activated = gelu_value(pre_act).astype(jnp.bfloat16)
    grad_pre = (grad_act * gelu_slope(pre_act)).astype(jnp.bfloat16)
    norm_part = contract_last(grad_pre, up_full).astype(jnp.bfloat16)
    ffn_part = contract_last(activated, down_turned).astype(jnp.bfloat16)
    norm_rows = scatter_sum(norm_part)
    out_rows = lax.dynamic_slice_in_dim(grad_output, row_start, rows_share, 0).astype(jnp.float32)
    grad_resid_rows = (out_rows + norm_back(resid_f, resid_scale, norm_rows)).astype(jnp.bfloat16)
    ffn_shares = ffn_part.reshape(SIDE, SIDE * rows_share, width)
    ffn_share = ring_sum_finish(ring_sum_start(ffn_shares, False), False)
    grad_resid, ffn_share = lax.optimization_barrier((gather_rows(grad_resid_rows), ffn_share))
    grad_mix = contract_last(grad_resid, output_weight).astype(jnp.bfloat16)
    mix_heads_grad = grad_mix.reshape(block_count, BLOCK, heads_here, HD)
    grad_probs = jnp.einsum(
        "cqhd,ckhd->chqk", mix_heads_grad, value_heads, preferred_element_type=jnp.float32
    )
    row_dot = jnp.einsum(
        "cqhd,cqhd->chq", mix_heads_grad, head_mix, preferred_element_type=jnp.float32
    )[..., None]
    grad_scores = (attention * (grad_probs - row_dot) * score_factor).astype(jnp.bfloat16)
    grad_query = (
        jnp.einsum("chqk,ckhd->cqhd", grad_scores, key_heads, preferred_element_type=jnp.float32)
        .astype(jnp.bfloat16)
        .reshape(token_count, head_width)
    )
    grad_keys = jnp.einsum(
        "chqk,cqhd->ckhd", grad_scores, query_heads, preferred_element_type=jnp.float32
    ).astype(jnp.bfloat16)
    grad_values = jnp.einsum(
        "chqk,cqhd->ckhd", attention_b, mix_heads_grad, preferred_element_type=jnp.float32
    ).astype(jnp.bfloat16)
    both_grads = jnp.concatenate([grad_keys, grad_values], axis=3).reshape(
        block_count, 2 * NLEN, 2 * head_width
    )
    enc_grad = jnp.concatenate(
        [
            sum(
                jnp.dot(
                    enc_parts[part][at],
                    both_grads[:, 2 * PART * part : 2 * PART * (part + 1)].reshape(
                        -1, 2 * head_width
                    ),
                    preferred_element_type=jnp.float32,
                )
                for part in range(part_count)
            ).astype(jnp.bfloat16)
            for at in range(2 * SIDE)
        ],
        axis=0,
    ).reshape(-1, half_block, 2 * head_width)
    places = jnp.sum(
        jnp.where(
            blocks.reshape(1, -1) == jnp.arange(blocks.size, dtype=jnp.int32)[:, None],
            jnp.arange(blocks.size, dtype=jnp.int32)[None, :],
            0,
        ),
        axis=1,
    ).reshape(data_size // 2, 2, 2)

    def shares_of(core):
        def rows_of(part):
            shares = part.reshape(data_size // 2, 2, -1, head_width)
            return lax.dynamic_index_in_dim(shares, core, 1, keepdims=False)

        places_here = lax.dynamic_index_in_dim(places, core, 1, keepdims=False)
        enc_share = jnp.take(enc_grad, places_here, axis=0, mode="clip").reshape(
            data_size // 2, -1, 2 * head_width
        )
        return jnp.stack(
            [
                rows_of(query_part),
                enc_share[:, :, :head_width],
                enc_share[:, :, head_width:],
                rows_of(mix_part),
            ],
            axis=1,
        )

    query_part = contract_first(normed, grad_query).astype(jnp.bfloat16)
    mix_part = contract_first(grad_resid, mix_rows).astype(jnp.bfloat16)
    summed, grad_query = data_sum(shares_of, grad_query)
    ffn_shares = ffn_share.reshape(SIDE, rows_share, width)
    ffn_rows_sum = ring_sum_finish(ring_sum_start(ffn_shares, True), True)
    summed = summed.astype(jnp.float32)
    query_grad, key_grad, value_grad = summed[0], summed[1], summed[2]
    mix_grad = summed[3].T
    input_part = contract_last(grad_query, query_weight)
    input_rows = scatter_sum(input_part)
    layer_out = (resid_f + ffn_rows_sum.astype(jnp.float32)).astype(jnp.bfloat16)
    grad_tokens = (
        grad_resid_rows.astype(jnp.float32) + norm_back(token_rows, base_rows, input_rows)
    ).astype(jnp.bfloat16)
    return (layer_out, grad_tokens, query_grad, key_grad, value_grad, mix_grad)


def solution(mesh):
    in_specs = (
        P("dp", None),
        P("dp", None, "tensor"),
        P("dp", None),
        P("dp", None),
        P(None, "tensor"),
        P(None, "tensor"),
        P(None, "tensor"),
        P("tensor", None),
        P("dp", "tensor"),
        P("tensor", "dp"),
        P("dp", None),
    )
    out_specs = (
        P(("dp", "tensor"), None),
        P(("dp", "tensor"), None),
        P("dp", "tensor"),
        P("dp", "tensor"),
        P("dp", "tensor"),
        P("tensor", "dp"),
    )
    return jax.shard_map(local, mesh=mesh, in_specs=in_specs, out_specs=out_specs, check_vma=False)
```

```python
import math

import jax
import jax.numpy as jnp
from jax import lax
from jax.sharding import PartitionSpec as P

HD = 128
BLOCK = 64
NLEN = 128
SIDE = 4
DATA = ("z", "core")
PLANE = ("y", "x")


epsilon = 1e-06
gelu_root = 0.7978845608028654
gelu_cubic = 0.044715


def rms_scale(values):
    return lax.rsqrt(jnp.mean(values * values, axis=-1, keepdims=True) + epsilon)


def norm_back(values, factor, incoming):
    normal_part = values * factor
    return (
        incoming - normal_part * jnp.mean(incoming * normal_part, axis=-1, keepdims=True)
    ) * factor


def gelu_value(inputs):
    inner = gelu_root * (inputs + gelu_cubic * inputs * inputs * inputs)
    return 0.5 * inputs * (1.0 + jnp.tanh(inner))


def gelu_slope(inputs):
    inner = gelu_root * (inputs + gelu_cubic * inputs * inputs * inputs)
    tanh_part = jnp.tanh(inner)
    return 0.5 * (1.0 + tanh_part) + 0.5 * inputs * (1.0 - tanh_part * tanh_part) * gelu_root * (
        1.0 + 3.0 * gelu_cubic * inputs * inputs
    )


def rounded(partial_value):
    return lax.optimization_barrier(partial_value.astype(jnp.bfloat16)).astype(jnp.float32)


def contract_last(left_side, right_side):
    return lax.dot_general(
        left_side, right_side, (((1,), (1,)), ((), ())), preferred_element_type=jnp.float32
    )


def contract_first(left_side, right_side):
    return lax.dot_general(
        left_side, right_side, (((0,), (0,)), ((), ())), preferred_element_type=jnp.float32
    )


def copies_to(rows, axis):
    size = lax.axis_size(axis)
    copies = jnp.broadcast_to(rows[None], (size,) + rows.shape)
    gathered = lax.all_to_all(copies, axis, split_axis=0, concat_axis=0, tiled=True)
    return gathered.reshape(size * rows.shape[0], rows.shape[1])


def scatter_sum(partial_rows, axis):
    size = lax.axis_size(axis)
    share = partial_rows.shape[0] // size
    swapped = lax.all_to_all(
        partial_rows.astype(jnp.bfloat16).reshape(size, share, partial_rows.shape[1]),
        axis,
        split_axis=0,
        concat_axis=0,
        tiled=True,
    )
    return jnp.sum(swapped.astype(jnp.float32), axis=0)


def heads_of_block(own_head_blocks):
    here = lax.axis_index("y")
    heads = lax.dynamic_update_index_in_dim(
        jnp.zeros_like(own_head_blocks),
        lax.dynamic_index_in_dim(own_head_blocks, here, 0, keepdims=False),
        here,
        0,
    )
    for step in range(1, SIDE):
        sent = lax.dynamic_index_in_dim(
            own_head_blocks, lax.rem(here + step, SIDE), 0, keepdims=False
        )
        got = lax.ppermute(
            sent, "y", [(place, (place + step) % SIDE) for place in range(SIDE)]
        )
        heads = lax.dynamic_update_index_in_dim(heads, got, lax.rem(here + SIDE - step, SIDE), 0)
    return heads


def data_sum(partial_rows, after):
    core = lax.axis_index("core")
    shares = partial_rows.reshape(lax.axis_size("z"), 2, -1, partial_rows.shape[1])
    given = lax.dynamic_index_in_dim(shares, 1 - core, 1, keepdims=False)
    kept = lax.dynamic_index_in_dim(shares, core, 1, keepdims=False)
    got = lax.ppermute(given, "core", [(0, 1), (1, 0)])
    paired = (kept.astype(jnp.float32) + got.astype(jnp.float32)).astype(jnp.bfloat16)
    paired, after = lax.optimization_barrier((paired, after))
    summed = lax.psum_scatter(
        paired.reshape(-1, paired.shape[2]), "z", scatter_dimension=0, tiled=True
    )
    return summed, after


def local(
    tokens,
    neighbour_buffer,
    shard_ids,
    row_ids,
    query_weight,
    key_weight,
    value_weight,
    output_weight,
    up_weight,
    down_weight,
    grad_output,
):
    data_size = lax.axis_size(DATA)
    tensor_size = lax.axis_size(PLANE)
    token_count = tokens.shape[0]
    width = tokens.shape[1]
    block_count = shard_ids.shape[0]
    capacity = block_count // 2
    pair_count = 2 * block_count
    owners = shard_ids.reshape(pair_count)
    wanted = row_ids.reshape(pair_count)
    same_owner = owners[:, None] == owners[None, :]
    earlier = lax.broadcasted_iota(jnp.int32, (pair_count, pair_count), 0) < lax.broadcasted_iota(
        jnp.int32, (pair_count, pair_count), 1
    )
    slot_index = jnp.sum((same_owner & earlier).astype(jnp.int32), axis=0)
    owner_grid = lax.broadcasted_iota(jnp.int32, (data_size, capacity, pair_count), 0)
    slot_grid = lax.broadcasted_iota(jnp.int32, (data_size, capacity, pair_count), 1)
    slot_match = (owners[None, None, :] == owner_grid) & (slot_index[None, None, :] == slot_grid)
    requests = jnp.sum(jnp.where(slot_match, wanted[None, None, :], 0), axis=2)
    asked = lax.all_to_all(requests, DATA, split_axis=0, concat_axis=0, tiled=True)
    replies = lax.all_to_all(
        jnp.take(neighbour_buffer, asked, axis=0, mode="clip"),
        DATA,
        split_axis=0,
        concat_axis=0,
        tiled=True,
    )
    reply_rows = replies.reshape((data_size * capacity,) + replies.shape[2:])
    mine = jnp.take(reply_rows, owners * capacity + slot_index, axis=0, mode="clip")
    enc_mine = mine.reshape(pair_count * NLEN, -1).T
    both_weights = lax.all_gather(
        jnp.concatenate([key_weight, value_weight], axis=1), "y", axis=0, tiled=False
    )
    output_heads = lax.all_gather(output_weight, "y", axis=0, tiled=True)
    token_f = tokens.astype(jnp.float32)
    base_scale = rms_scale(token_f)
    normed = (token_f * base_scale).astype(jnp.bfloat16)
    query_rows = jnp.dot(normed, query_weight, preferred_element_type=jnp.float32).astype(
        jnp.bfloat16
    )
    query_heads = heads_of_block(query_rows.reshape(block_count, BLOCK, HD))
    enc_mine, both_weights, query_heads = lax.optimization_barrier(
        (enc_mine, both_weights, query_heads)
    )
    features, enc_columns = enc_mine.shape
    keys_here = 2 * NLEN
    block_pieces = jnp.swapaxes(enc_mine.reshape(features, SIDE, keys_here), 0, 1)
    enc_block = lax.all_to_all(
        jnp.broadcast_to(
            block_pieces[:, None], (SIDE, SIDE, features, keys_here)
        ).reshape(SIDE * SIDE, features, keys_here),
        PLANE,
        split_axis=0,
        concat_axis=0,
        tiled=True,
    ).reshape(width, keys_here)
    frozen = jnp.concatenate([up_weight, down_weight.T], axis=1)
    enc_block, output_heads, frozen = lax.optimization_barrier((enc_block, output_heads, frozen))
    frozen_full = lax.all_gather(frozen, DATA, axis=0, tiled=True)
    hidden = up_weight.shape[1]
    up_full = frozen_full[:, :hidden]
    down_turned = frozen_full[:, hidden:]
    both_heads = jnp.stack(
        [
            contract_first(enc_block, both_weights[head]).astype(jnp.bfloat16)
            for head in range(SIDE)
        ]
    )
    key_heads = both_heads[:, :, :HD]
    value_heads = both_heads[:, :, HD:]
    score_factor = 1.0 / math.sqrt(HD)
    scores = (
        jnp.einsum("hqd,hkd->hqk", query_heads, key_heads, preferred_element_type=jnp.float32)
        * score_factor
    )
    raised = jnp.exp(scores)
    attention = raised / jnp.sum(raised, axis=-1, keepdims=True)
    attention_b = attention.astype(jnp.bfloat16)
    head_mix = jnp.einsum(
        "hqk,hkd->hqd", attention_b, value_heads, preferred_element_type=jnp.float32
    ).astype(jnp.bfloat16)
    mix_rows = jnp.swapaxes(head_mix, 0, 1).reshape(BLOCK, SIDE * HD)
    attn_part = jnp.dot(mix_rows, output_heads, preferred_element_type=jnp.float32)
    rows_share = token_count // tensor_size
    row_start = lax.axis_index(PLANE) * rows_share
    token_rows = lax.dynamic_slice_in_dim(tokens, row_start, rows_share, 0).astype(jnp.float32)
    base_rows = lax.dynamic_slice_in_dim(base_scale, row_start, rows_share, 0)
    attn_rows, enc_mine = lax.optimization_barrier((scatter_sum(attn_part, "x"), enc_mine))
    enc_full = lax.all_gather(enc_mine, PLANE, axis=0, tiled=True)
    resid_f = rounded(token_rows + attn_rows)
    resid_scale = rms_scale(resid_f)
    ffn_in = copies_to((resid_f * resid_scale).astype(jnp.bfloat16), PLANE)
    grad_act = lax.optimization_barrier(
        jnp.dot(grad_output, down_turned, preferred_element_type=jnp.float32)
    )
    pre_act = jnp.dot(ffn_in, up_full, preferred_element_type=jnp.float32)
    activated = gelu_value(pre_act).astype(jnp.bfloat16)
    grad_pre = (grad_act * gelu_slope(pre_act)).astype(jnp.bfloat16)
    norm_part = contract_last(grad_pre, up_full)
    ffn_part = contract_last(activated, down_turned).astype(jnp.bfloat16)
    norm_rows = scatter_sum(norm_part, PLANE)
    out_rows = lax.dynamic_slice_in_dim(grad_output, row_start, rows_share, 0).astype(jnp.float32)
    grad_resid_rows = (out_rows + norm_back(resid_f, resid_scale, norm_rows)).astype(jnp.bfloat16)
    grad_block = copies_to(grad_resid_rows, "x")
    grad_resid = lax.all_gather(grad_block, "y", axis=0, tiled=True)
    grad_mix = contract_last(grad_block, output_heads).astype(jnp.bfloat16)
    mix_heads_grad = jnp.swapaxes(grad_mix.reshape(BLOCK, SIDE, HD), 0, 1)
    grad_probs = jnp.einsum(
        "hqd,hkd->hqk", mix_heads_grad, value_heads, preferred_element_type=jnp.float32
    )
    row_dot = jnp.einsum(
        "hqd,hqd->hq", mix_heads_grad, head_mix, preferred_element_type=jnp.float32
    )[..., None]
    grad_scores = (attention * (grad_probs - row_dot) * score_factor).astype(jnp.bfloat16)
    grad_query = jnp.einsum(
        "hqk,hkd->hqd", grad_scores, key_heads, preferred_element_type=jnp.float32
    ).astype(jnp.bfloat16)
    grad_keys = jnp.einsum(
        "hqk,hqd->hkd", grad_scores, query_heads, preferred_element_type=jnp.float32
    ).astype(jnp.bfloat16)
    grad_values = jnp.einsum(
        "hqk,hqd->hkd", attention_b, mix_heads_grad, preferred_element_type=jnp.float32
    ).astype(jnp.bfloat16)
    swapped = lax.all_to_all(
        jnp.concatenate([grad_keys, grad_values, grad_query, head_mix], axis=1),
        "y",
        split_axis=0,
        concat_axis=0,
        tiled=True,
    )
    swapped, ffn_part = lax.optimization_barrier((swapped, ffn_part))
    both_grads = jnp.concatenate(
        [
            swapped[:, :keys_here].reshape(enc_columns, HD),
            swapped[:, keys_here : 2 * keys_here].reshape(enc_columns, HD),
        ],
        axis=1,
    )
    query_grads = swapped[:, 2 * keys_here : 2 * keys_here + BLOCK].reshape(token_count, HD)
    mix_back = swapped[:, 2 * keys_here + BLOCK :].reshape(token_count, HD)
    weight_parts = jnp.concatenate(
        [
            contract_first(normed, query_grads),
            jnp.dot(enc_full, both_grads, preferred_element_type=jnp.float32),
            contract_first(grad_resid, mix_back),
        ],
        axis=1,
    ).astype(jnp.bfloat16)
    summed, query_grads = data_sum(weight_parts, query_grads)
    summed = summed.astype(jnp.float32)
    query_grad = summed[:, :HD]
    key_grad = summed[:, HD : 2 * HD]
    value_grad = summed[:, 2 * HD : 3 * HD]
    mix_grad = summed[:, 3 * HD :].T
    layer_out = (resid_f + scatter_sum(ffn_part, PLANE)).astype(jnp.bfloat16)
    input_part = contract_last(query_grads, query_weight)
    input_rows = scatter_sum(input_part, PLANE)
    grad_tokens = (
        grad_resid_rows.astype(jnp.float32) + norm_back(token_rows, base_rows, input_rows)
    ).astype(jnp.bfloat16)
    return (layer_out, grad_tokens, query_grad, key_grad, value_grad, mix_grad)


def solution(mesh):
    mesh = jax.sharding.Mesh(
        mesh.devices.reshape(-1, 2, SIDE, SIDE), DATA + PLANE
    )
    in_specs = (
        P(DATA, None),
        P(DATA, None, PLANE),
        P(DATA, None),
        P(DATA, None),
        P(None, PLANE),
        P(None, PLANE),
        P(None, PLANE),
        P(PLANE, None),
        P(DATA, PLANE),
        P(PLANE, DATA),
        P(DATA, None),
    )
    out_specs = (
        P(DATA + PLANE, None),
        P(DATA + PLANE, None),
        P(DATA, PLANE),
        P(DATA, PLANE),
        P(DATA, PLANE),
        P(PLANE, DATA),
    )
    return jax.shard_map(local, mesh=mesh, in_specs=in_specs, out_specs=out_specs, check_vma=False)
```

```python
import math

import jax
import jax.numpy as jnp
from jax import lax
from jax.sharding import PartitionSpec as P

HD = 128
BLOCK = 64
NLEN = 128
SIDE = 4
DATA = ("z", "core")
PLANE = ("y", "x")
ORDER = (0, -1, 1, 2)


epsilon = 1e-06
gelu_root = 0.7978845608028654
gelu_cubic = 0.044715


def rms_scale(values):
    return lax.rsqrt(jnp.mean(values * values, axis=-1, keepdims=True) + epsilon)


def norm_back(values, factor, incoming):
    normal_part = values * factor
    return (
        incoming - normal_part * jnp.mean(incoming * normal_part, axis=-1, keepdims=True)
    ) * factor


def gelu_value(inputs):
    inner = gelu_root * (inputs + gelu_cubic * inputs * inputs * inputs)
    return 0.5 * inputs * (1.0 + jnp.tanh(inner))


def gelu_slope(inputs):
    inner = gelu_root * (inputs + gelu_cubic * inputs * inputs * inputs)
    tanh_part = jnp.tanh(inner)
    return 0.5 * (1.0 + tanh_part) + 0.5 * inputs * (1.0 - tanh_part * tanh_part) * gelu_root * (
        1.0 + 3.0 * gelu_cubic * inputs * inputs
    )


def rounded(partial_value):
    return lax.optimization_barrier(partial_value.astype(jnp.bfloat16)).astype(jnp.float32)


def contract_last(left_side, right_side):
    return lax.dot_general(
        left_side, right_side, (((1,), (1,)), ((), ())), preferred_element_type=jnp.float32
    )


def contract_first(left_side, right_side):
    return lax.dot_general(
        left_side, right_side, (((0,), (0,)), ((), ())), preferred_element_type=jnp.float32
    )


def copies_to(rows, axis):
    size = lax.axis_size(axis)
    copies = jnp.broadcast_to(rows[None], (size,) + rows.shape)
    gathered = lax.all_to_all(copies, axis, split_axis=0, concat_axis=0, tiled=True)
    return gathered.reshape(size * rows.shape[0], rows.shape[1])


def scatter_sum(partial_rows, axis):
    size = lax.axis_size(axis)
    share = partial_rows.shape[0] // size
    swapped = lax.all_to_all(
        partial_rows.astype(jnp.bfloat16).reshape(size, share, partial_rows.shape[1]),
        axis,
        split_axis=0,
        concat_axis=0,
        tiled=True,
    )
    return jnp.sum(swapped.astype(jnp.float32), axis=0)


def heads_of_block(own_head_blocks):
    here = lax.axis_index("y")
    heads = lax.dynamic_update_index_in_dim(
        jnp.zeros_like(own_head_blocks),
        lax.dynamic_index_in_dim(own_head_blocks, here, 0, keepdims=False),
        here,
        0,
    )
    for step in range(1, SIDE):
        sent = lax.dynamic_index_in_dim(
            own_head_blocks, lax.rem(here + step, SIDE), 0, keepdims=False
        )
        got = lax.ppermute(
            sent, "y", [(place, (place + step) % SIDE) for place in range(SIDE)]
        )
        heads = lax.dynamic_update_index_in_dim(heads, got, lax.rem(here + SIDE - step, SIDE), 0)
    return heads


def ring_shift(piece, step):
    return lax.ppermute(
        piece, "y", [(place, (place + step) % SIDE) for place in range(SIDE)]
    )


def ring_parts(piece, before, behind):
    half = piece.shape[0] // 2
    opposite = [ring_shift(before[:half], 1), ring_shift(behind[half:], -1)]
    return jnp.concatenate([piece, before, behind] + opposite, axis=0)


def data_sum(partial_rows, after):
    core = lax.axis_index("core")
    shares = partial_rows.reshape(lax.axis_size("z"), 2, -1, partial_rows.shape[1])
    given = lax.dynamic_index_in_dim(shares, 1 - core, 1, keepdims=False)
    kept = lax.dynamic_index_in_dim(shares, core, 1, keepdims=False)
    got = lax.ppermute(given, "core", [(0, 1), (1, 0)])
    paired = (kept.astype(jnp.float32) + got.astype(jnp.float32)).astype(jnp.bfloat16)
    paired, after = lax.optimization_barrier((paired, after))
    summed = lax.psum_scatter(
        paired.reshape(-1, paired.shape[2]), "z", scatter_dimension=0, tiled=True
    )
    return summed, after


def local(
    tokens,
    neighbour_buffer,
    shard_ids,
    row_ids,
    query_weight,
    key_weight,
    value_weight,
    output_weight,
    up_weight,
    down_weight,
    grad_output,
):
    data_size = lax.axis_size(DATA)
    tensor_size = lax.axis_size(PLANE)
    token_count = tokens.shape[0]
    width = tokens.shape[1]
    block_count = shard_ids.shape[0]
    capacity = block_count // 2
    pair_count = 2 * block_count
    owners = shard_ids.reshape(pair_count)
    wanted = row_ids.reshape(pair_count)
    same_owner = owners[:, None] == owners[None, :]
    earlier = lax.broadcasted_iota(jnp.int32, (pair_count, pair_count), 0) < lax.broadcasted_iota(
        jnp.int32, (pair_count, pair_count), 1
    )
    slot_index = jnp.sum((same_owner & earlier).astype(jnp.int32), axis=0)
    owner_grid = lax.broadcasted_iota(jnp.int32, (data_size, capacity, pair_count), 0)
    slot_grid = lax.broadcasted_iota(jnp.int32, (data_size, capacity, pair_count), 1)
    slot_match = (owners[None, None, :] == owner_grid) & (slot_index[None, None, :] == slot_grid)
    requests = jnp.sum(jnp.where(slot_match, wanted[None, None, :], 0), axis=2)
    asked = lax.all_to_all(requests, DATA, split_axis=0, concat_axis=0, tiled=True)
    replies = lax.all_to_all(
        jnp.take(neighbour_buffer, asked, axis=0, mode="clip"),
        DATA,
        split_axis=0,
        concat_axis=0,
        tiled=True,
    )
    reply_rows = replies.reshape((data_size * capacity,) + replies.shape[2:])
    mine = jnp.take(reply_rows, owners * capacity + slot_index, axis=0, mode="clip")
    enc_mine = mine.reshape(pair_count * NLEN, -1).T
    both_weights = lax.all_gather(
        jnp.concatenate([key_weight, value_weight], axis=1), "y", axis=0, tiled=False
    )
    output_before, output_behind = ring_shift(output_weight, 1), ring_shift(output_weight, -1)
    here = lax.axis_index("y")
    ring_heads = lax.rem(here + jnp.array(ORDER, jnp.int32) + SIDE, SIDE)
    ring_places = jnp.take(
        jnp.array([ORDER.index(step) for step in (0, 1, 2, -1)], jnp.int32),
        lax.rem(jnp.arange(SIDE, dtype=jnp.int32) - here + SIDE, SIDE),
        mode="clip",
    )
    token_f = tokens.astype(jnp.float32)
    base_scale = rms_scale(token_f)
    normed = (token_f * base_scale).astype(jnp.bfloat16)
    query_rows = jnp.dot(normed, query_weight, preferred_element_type=jnp.float32).astype(
        jnp.bfloat16
    )
    query_heads = heads_of_block(query_rows.reshape(block_count, BLOCK, HD))
    frozen = jnp.concatenate([up_weight, down_weight.T], axis=1)
    enc_mine, query_heads, frozen, output_before, output_behind = lax.optimization_barrier(
        (enc_mine, query_heads, frozen, output_before, output_behind)
    )
    output_heads = ring_parts(output_weight, output_before, output_behind)
    features, enc_columns = enc_mine.shape
    keys_here = 2 * NLEN
    block_pieces = jnp.swapaxes(enc_mine.reshape(features, SIDE, keys_here), 0, 1)
    enc_block = lax.all_to_all(
        jnp.broadcast_to(
            block_pieces[:, None], (SIDE, SIDE, features, keys_here)
        ).reshape(SIDE * SIDE, features, keys_here),
        PLANE,
        split_axis=0,
        concat_axis=0,
        tiled=True,
    ).reshape(width, keys_here)
    enc_block, both_weights, output_heads = lax.optimization_barrier(
        (enc_block, both_weights, output_heads)
    )
    frozen_full = lax.all_gather(frozen, DATA, axis=0, tiled=True)
    hidden = up_weight.shape[1]
    up_full = frozen_full[:, :hidden]
    down_turned = frozen_full[:, hidden:]
    both_heads = jnp.stack(
        [
            contract_first(enc_block, both_weights[head]).astype(jnp.bfloat16)
            for head in range(SIDE)
        ]
    )
    key_heads = both_heads[:, :, :HD]
    value_heads = both_heads[:, :, HD:]
    score_factor = 1.0 / math.sqrt(HD)
    scores = (
        jnp.einsum("hqd,hkd->hqk", query_heads, key_heads, preferred_element_type=jnp.float32)
        * score_factor
    )
    raised = jnp.exp(scores)
    attention = raised / jnp.sum(raised, axis=-1, keepdims=True)
    attention_b = attention.astype(jnp.bfloat16)
    head_mix = jnp.einsum(
        "hqk,hkd->hqd", attention_b, value_heads, preferred_element_type=jnp.float32
    ).astype(jnp.bfloat16)
    mix_rows = jnp.swapaxes(
        jnp.take(head_mix, ring_heads, axis=0, mode="clip"), 0, 1
    ).reshape(BLOCK, SIDE * HD)
    attn_part = jnp.dot(mix_rows, output_heads, preferred_element_type=jnp.float32)
    rows_share = token_count // tensor_size
    row_start = lax.axis_index(PLANE) * rows_share
    token_rows = lax.dynamic_slice_in_dim(tokens, row_start, rows_share, 0).astype(jnp.float32)
    base_rows = lax.dynamic_slice_in_dim(base_scale, row_start, rows_share, 0)
    attn_rows, enc_mine = lax.optimization_barrier((scatter_sum(attn_part, "x"), enc_mine))
    enc_full = lax.all_gather(enc_mine, PLANE, axis=0, tiled=True)
    resid_f = rounded(token_rows + attn_rows)
    resid_scale = rms_scale(resid_f)
    ffn_in = copies_to((resid_f * resid_scale).astype(jnp.bfloat16), PLANE)
    grad_act = lax.optimization_barrier(
        jnp.dot(grad_output, down_turned, preferred_element_type=jnp.float32)
    )
    pre_act = jnp.dot(ffn_in, up_full, preferred_element_type=jnp.float32)
    activated = gelu_value(pre_act).astype(jnp.bfloat16)
    grad_pre = (grad_act * gelu_slope(pre_act)).astype(jnp.bfloat16)
    norm_part = contract_last(grad_pre, up_full)
    ffn_part = contract_last(activated, down_turned).astype(jnp.bfloat16)
    norm_rows = scatter_sum(norm_part, PLANE)
    out_rows = lax.dynamic_slice_in_dim(grad_output, row_start, rows_share, 0).astype(jnp.float32)
    grad_resid_rows = (out_rows + norm_back(resid_f, resid_scale, norm_rows)).astype(jnp.bfloat16)
    grad_block, enc_full = lax.optimization_barrier((copies_to(grad_resid_rows, "x"), enc_full))
    grad_resid = lax.all_gather(grad_block, "y", axis=0, tiled=True)
    grad_mix = contract_last(grad_block, output_heads).astype(jnp.bfloat16)
    mix_heads_grad = jnp.take(
        jnp.swapaxes(grad_mix.reshape(BLOCK, SIDE, HD), 0, 1), ring_places, axis=0, mode="clip"
    )
    grad_probs = jnp.einsum(
        "hqd,hkd->hqk", mix_heads_grad, value_heads, preferred_element_type=jnp.float32
    )
    row_dot = jnp.einsum(
        "hqd,hqd->hq", mix_heads_grad, head_mix, preferred_element_type=jnp.float32
    )[..., None]
    grad_scores = (attention * (grad_probs - row_dot) * score_factor).astype(jnp.bfloat16)
    grad_query = jnp.einsum(
        "hqk,hkd->hqd", grad_scores, key_heads, preferred_element_type=jnp.float32
    ).astype(jnp.bfloat16)
    grad_keys = jnp.einsum(
        "hqk,hqd->hkd", grad_scores, query_heads, preferred_element_type=jnp.float32
    ).astype(jnp.bfloat16)
    grad_values = jnp.einsum(
        "hqk,hqd->hkd", attention_b, mix_heads_grad, preferred_element_type=jnp.float32
    ).astype(jnp.bfloat16)
    swapped = lax.all_to_all(
        jnp.concatenate([grad_keys, grad_values, grad_query, head_mix], axis=1),
        "y",
        split_axis=0,
        concat_axis=0,
        tiled=True,
    )
    swapped, ffn_part = lax.optimization_barrier((swapped, ffn_part))
    both_grads = jnp.concatenate(
        [
            swapped[:, :keys_here].reshape(enc_columns, HD),
            swapped[:, keys_here : 2 * keys_here].reshape(enc_columns, HD),
        ],
        axis=1,
    )
    query_grads = swapped[:, 2 * keys_here : 2 * keys_here + BLOCK].reshape(token_count, HD)
    mix_back = swapped[:, 2 * keys_here + BLOCK :].reshape(token_count, HD)
    weight_parts = jnp.concatenate(
        [
            contract_first(normed, query_grads),
            jnp.dot(enc_full, both_grads, preferred_element_type=jnp.float32),
            contract_first(grad_resid, mix_back),
        ],
        axis=1,
    ).astype(jnp.bfloat16)
    summed, query_grads = data_sum(weight_parts, query_grads)
    summed = summed.astype(jnp.float32)
    query_grad = summed[:, :HD]
    key_grad = summed[:, HD : 2 * HD]
    value_grad = summed[:, 2 * HD : 3 * HD]
    mix_grad = summed[:, 3 * HD :].T
    layer_out = (resid_f + scatter_sum(ffn_part, PLANE)).astype(jnp.bfloat16)
    input_part = contract_last(query_grads, query_weight)
    input_rows = scatter_sum(input_part, PLANE)
    grad_tokens = (
        grad_resid_rows.astype(jnp.float32) + norm_back(token_rows, base_rows, input_rows)
    ).astype(jnp.bfloat16)
    return (layer_out, grad_tokens, query_grad, key_grad, value_grad, mix_grad)


def solution(mesh):
    mesh = jax.sharding.Mesh(
        mesh.devices.reshape(-1, 2, SIDE, SIDE), DATA + PLANE
    )
    in_specs = (
        P(DATA, None),
        P(DATA, None, PLANE),
        P(DATA, None),
        P(DATA, None),
        P(None, PLANE),
        P(None, PLANE),
        P(None, PLANE),
        P(PLANE, None),
        P(DATA, PLANE),
        P(PLANE, DATA),
        P(DATA, None),
    )
    out_specs = (
        P(DATA + PLANE, None),
        P(DATA + PLANE, None),
        P(DATA, PLANE),
        P(DATA, PLANE),
        P(DATA, PLANE),
        P(PLANE, DATA),
    )
    return jax.shard_map(local, mesh=mesh, in_specs=in_specs, out_specs=out_specs, check_vma=False)
```

```python
import math

import jax
import jax.numpy as jnp
from jax import lax
from jax.experimental import pallas as pl
from jax.experimental.pallas import tpu as pltpu
from jax.sharding import PartitionSpec as P

HD = 128
BLOCK = 64
NLEN = 128
SIDE = 4
DATA = ("z", "core")
PLANE = ("yh", "yl", "x")
EIGHT = ("yh", "x")


epsilon = 1e-06
gelu_root = 0.7978845608028654
gelu_cubic = 0.044715


def rms_scale(values):
    return lax.rsqrt(jnp.mean(values * values, axis=-1, keepdims=True) + epsilon)


def norm_back(values, factor, incoming):
    normal_part = values * factor
    return (
        incoming - normal_part * jnp.mean(incoming * normal_part, axis=-1, keepdims=True)
    ) * factor


def gelu_value(inputs):
    inner = gelu_root * (inputs + gelu_cubic * inputs * inputs * inputs)
    return 0.5 * inputs * (1.0 + jnp.tanh(inner))


def gelu_slope(inputs):
    inner = gelu_root * (inputs + gelu_cubic * inputs * inputs * inputs)
    tanh_part = jnp.tanh(inner)
    return 0.5 * (1.0 + tanh_part) + 0.5 * inputs * (1.0 - tanh_part * tanh_part) * gelu_root * (
        1.0 + 3.0 * gelu_cubic * inputs * inputs
    )


def rounded(partial_value):
    return lax.optimization_barrier(partial_value.astype(jnp.bfloat16)).astype(jnp.float32)


def contract_last(left_side, right_side):
    return lax.dot_general(
        left_side, right_side, (((1,), (1,)), ((), ())), preferred_element_type=jnp.float32
    )


def contract_first(left_side, right_side):
    return lax.dot_general(
        left_side, right_side, (((0,), (0,)), ((), ())), preferred_element_type=jnp.float32
    )


def copies_to(rows, axis):
    size = lax.axis_size(axis)
    copies = jnp.broadcast_to(rows[None], (size,) + rows.shape)
    gathered = lax.all_to_all(copies, axis, split_axis=0, concat_axis=0, tiled=True)
    return gathered.reshape(size * rows.shape[0], rows.shape[1])


def scatter_sum(partial_rows, axis):
    size = lax.axis_size(axis)
    share = partial_rows.shape[0] // size
    swapped = lax.all_to_all(
        partial_rows.astype(jnp.bfloat16).reshape(size, share, partial_rows.shape[1]),
        axis,
        split_axis=0,
        concat_axis=0,
        tiled=True,
    )
    return jnp.sum(swapped.astype(jnp.float32), axis=0)


def in_pair_order(own, other, axis):
    first = lax.axis_index("yl") == 0
    return jnp.where(first, jnp.stack([own, other], axis), jnp.stack([other, own], axis))


def pair_swap(given):
    return lax.ppermute(given, "yl", [(0, 1), (1, 0)])


FEATURES = 256
DEPTH = 512


def weight_grads_kernel(
    core, enc, normed, grad_own, grad_other, both_grads, query_grads, mix_own, mix_other, given, kept
):
    step = pl.program_id(0)
    rows = jnp.concatenate(
        [
            contract_first(normed[...], query_grads[...]),
            jnp.dot(enc[...], both_grads[...], preferred_element_type=jnp.float32),
            contract_first(grad_own[...], mix_own[...])
            + contract_first(grad_other[...], mix_other[...]),
        ],
        axis=1,
    ).astype(jnp.bfloat16)
    mine = lax.rem(step, 2) == core[0]

    @pl.when(mine)
    def _():
        kept[0] = rows

    @pl.when(jnp.logical_not(mine))
    def _():
        given[0] = rows


def weight_grads(enc, normed, grad_own, grad_other, both_grads, query_grads, mix_own, mix_other):
    width, enc_columns = enc.shape
    token_count = normed.shape[0]
    blocks = width // FEATURES
    columns = both_grads.shape[1] + query_grads.shape[1] + mix_own.shape[1]
    out_spec = pl.BlockSpec((1, FEATURES, columns), lambda step, core: (step // 2, 0, 0))
    out_shape = jax.ShapeDtypeStruct((blocks // 2, FEATURES, columns), jnp.bfloat16)
    return pl.pallas_call(
        weight_grads_kernel,
        grid_spec=pltpu.PrefetchScalarGridSpec(
            num_scalar_prefetch=1,
            grid=(blocks,),
            in_specs=[
                pl.BlockSpec((FEATURES, enc_columns), lambda step, core: (step, 0)),
                pl.BlockSpec((token_count, FEATURES), lambda step, core: (0, step)),
                pl.BlockSpec((grad_own.shape[0], FEATURES), lambda step, core: (0, step)),
                pl.BlockSpec((grad_own.shape[0], FEATURES), lambda step, core: (0, step)),
                pl.BlockSpec(both_grads.shape, lambda step, core: (0, 0)),
                pl.BlockSpec(query_grads.shape, lambda step, core: (0, 0)),
                pl.BlockSpec(mix_own.shape, lambda step, core: (0, 0)),
                pl.BlockSpec(mix_own.shape, lambda step, core: (0, 0)),
            ],
            out_specs=[out_spec, out_spec],
        ),
        out_shape=[out_shape, out_shape],
        cost_estimate=pl.CostEstimate(
            flops=2 * width * (enc_columns * 2 + token_count * 2) * HD,
            bytes_accessed=2 * width * (enc_columns + 2 * token_count + columns),
            transcendentals=0,
        ),
        compiler_params=pltpu.CompilerParams(vmem_limit_bytes=24 * 1024 * 1024),
    )(
        lax.axis_index("core").astype(jnp.int32).reshape(1),
        enc,
        normed,
        grad_own,
        grad_other,
        both_grads,
        query_grads,
        mix_own,
        mix_other,
    )


def project_kernel(enc, weights, out, total):
    step = pl.program_id(0)

    @pl.when(step == 0)
    def _():
        total[...] = jnp.zeros_like(total)

    turned = enc[...].T
    for head in range(weights.shape[0]):
        total[head] += jnp.dot(turned, weights[head], preferred_element_type=jnp.float32)

    @pl.when(step == pl.num_programs(0) - 1)
    def _():
        out[...] = total[...].astype(out.dtype)


def project(enc, weights):
    width, rows = enc.shape
    heads, _, columns = weights.shape
    return pl.pallas_call(
        project_kernel,
        grid=(width // DEPTH,),
        in_specs=[
            pl.BlockSpec((DEPTH, rows), lambda step: (step, 0)),
            pl.BlockSpec((heads, DEPTH, columns), lambda step: (0, step, 0)),
        ],
        out_specs=pl.BlockSpec((heads, rows, columns), lambda step: (0, 0, 0)),
        out_shape=jax.ShapeDtypeStruct((heads, rows, columns), jnp.bfloat16),
        scratch_shapes=[pltpu.VMEM((heads, rows, columns), jnp.float32)],
        cost_estimate=pl.CostEstimate(
            flops=2 * width * rows * heads * columns,
            bytes_accessed=2 * width * (rows + heads * columns),
            transcendentals=0,
        ),
        compiler_params=pltpu.CompilerParams(vmem_limit_bytes=24 * 1024 * 1024),
    )(enc, weights)


def data_sum(given, kept, after):
    got = lax.ppermute(given, "core", [(0, 1), (1, 0)])
    paired = (kept.astype(jnp.float32) + got.astype(jnp.float32)).astype(jnp.bfloat16)
    paired, after = lax.optimization_barrier((paired, after))
    summed = lax.psum_scatter(
        paired.reshape(-1, paired.shape[2]), "z", scatter_dimension=0, tiled=True
    )
    return summed, after


def local(
    tokens,
    neighbour_buffer,
    shard_ids,
    row_ids,
    query_weight,
    key_weight,
    value_weight,
    output_weight,
    up_weight,
    down_weight,
    grad_output,
):
    data_size = lax.axis_size(DATA)
    tensor_size = lax.axis_size(PLANE)
    token_count = tokens.shape[0]
    width = tokens.shape[1]
    block_count = shard_ids.shape[0]
    capacity = block_count // 2
    pair_count = 2 * block_count
    owners = shard_ids.reshape(pair_count)
    wanted = row_ids.reshape(pair_count)
    same_owner = owners[:, None] == owners[None, :]
    earlier = lax.broadcasted_iota(jnp.int32, (pair_count, pair_count), 0) < lax.broadcasted_iota(
        jnp.int32, (pair_count, pair_count), 1
    )
    slot_index = jnp.sum((same_owner & earlier).astype(jnp.int32), axis=0)
    owner_grid = lax.broadcasted_iota(jnp.int32, (data_size, capacity, pair_count), 0)
    slot_grid = lax.broadcasted_iota(jnp.int32, (data_size, capacity, pair_count), 1)
    slot_match = (owners[None, None, :] == owner_grid) & (slot_index[None, None, :] == slot_grid)
    requests = jnp.sum(jnp.where(slot_match, wanted[None, None, :], 0), axis=2)
    asked = lax.all_to_all(requests, DATA, split_axis=0, concat_axis=0, tiled=True)
    replies = lax.all_to_all(
        jnp.take(neighbour_buffer, asked, axis=0, mode="clip"),
        DATA,
        split_axis=0,
        concat_axis=0,
        tiled=True,
    )
    reply_rows = replies.reshape((data_size * capacity,) + replies.shape[2:])
    mine = jnp.take(reply_rows, owners * capacity + slot_index, axis=0, mode="clip")
    enc_mine = mine.reshape(pair_count * NLEN, -1).T
    both_weights = lax.all_gather(
        jnp.concatenate([key_weight, value_weight], axis=1), "yl", axis=0, tiled=False
    )
    output_heads = lax.all_gather(output_weight, "yl", axis=0, tiled=True)
    pair_place = lax.axis_index("yl")
    token_f = tokens.astype(jnp.float32)
    base_scale = rms_scale(token_f)
    normed = (token_f * base_scale).astype(jnp.bfloat16)
    query_rows = jnp.dot(normed, query_weight, preferred_element_type=jnp.float32).astype(
        jnp.bfloat16
    )
    query_blocks = query_rows.reshape(2, 2, BLOCK, HD)

    def of_class(blocks, axis, place):
        return lax.dynamic_index_in_dim(blocks, place, axis, keepdims=False)

    query_heads = in_pair_order(
        of_class(query_blocks, 1, pair_place),
        pair_swap(of_class(query_blocks, 1, 1 - pair_place)),
        0,
    )
    frozen = jnp.concatenate([up_weight, down_weight.T], axis=1)
    enc_mine, query_heads, frozen = lax.optimization_barrier((enc_mine, query_heads, frozen))
    features, enc_columns = enc_mine.shape
    keys_here = 2 * NLEN
    class_pieces = enc_mine.reshape(features, 2, 2, keys_here).transpose(2, 0, 1, 3)
    enc_block = lax.all_to_all(
        jnp.broadcast_to(
            class_pieces.reshape(1, 2, 1, features, 2 * keys_here),
            (2, 2, SIDE, features, 2 * keys_here),
        ).reshape(tensor_size, features, 2 * keys_here),
        PLANE,
        split_axis=0,
        concat_axis=0,
        tiled=True,
    ).reshape(width, 2 * keys_here)
    enc_block, both_weights, output_heads = lax.optimization_barrier(
        (enc_block, both_weights, output_heads)
    )
    frozen_full = lax.all_gather(frozen, DATA, axis=0, tiled=True)
    hidden = up_weight.shape[1]
    up_full = frozen_full[:, :hidden]
    down_turned = frozen_full[:, hidden:]
    both_heads = project(enc_block, both_weights).reshape(4, keys_here, 2 * HD)
    query_heads = query_heads.reshape(4, BLOCK, HD)
    key_heads = both_heads[:, :, :HD]
    value_heads = both_heads[:, :, HD:]
    score_factor = 1.0 / math.sqrt(HD)
    scores = (
        jnp.einsum("hqd,hkd->hqk", query_heads, key_heads, preferred_element_type=jnp.float32)
        * score_factor
    )
    raised = jnp.exp(scores)
    attention = raised / jnp.sum(raised, axis=-1, keepdims=True)
    attention_b = attention.astype(jnp.bfloat16)
    head_mix = jnp.einsum(
        "hqk,hkd->hqd", attention_b, value_heads, preferred_element_type=jnp.float32
    ).astype(jnp.bfloat16)
    mix_rows = head_mix.reshape(2, 2, BLOCK, HD).transpose(1, 2, 0, 3).reshape(2 * BLOCK, 2 * HD)
    attn_part = jnp.dot(mix_rows, output_heads, preferred_element_type=jnp.float32)
    rows_share = token_count // tensor_size
    row_start = lax.axis_index(PLANE) * rows_share
    token_rows = lax.dynamic_slice_in_dim(tokens, row_start, rows_share, 0).astype(jnp.float32)
    base_rows = lax.dynamic_slice_in_dim(base_scale, row_start, rows_share, 0)
    attn_rows, enc_mine = lax.optimization_barrier((scatter_sum(attn_part, EIGHT), enc_mine))
    enc_full = lax.all_gather(enc_mine, PLANE, axis=0, tiled=True)
    resid_f = rounded(token_rows + attn_rows)
    resid_scale = rms_scale(resid_f)
    ffn_in = copies_to((resid_f * resid_scale).astype(jnp.bfloat16), PLANE)
    grad_act = lax.optimization_barrier(
        jnp.dot(grad_output, down_turned, preferred_element_type=jnp.float32)
    )
    pre_act = jnp.dot(ffn_in, up_full, preferred_element_type=jnp.float32)
    activated = gelu_value(pre_act).astype(jnp.bfloat16)
    grad_pre = (grad_act * gelu_slope(pre_act)).astype(jnp.bfloat16)
    norm_part = contract_last(grad_pre, up_full)
    ffn_part = contract_last(activated, down_turned).astype(jnp.bfloat16)
    norm_rows = scatter_sum(norm_part, PLANE)
    out_rows = lax.dynamic_slice_in_dim(grad_output, row_start, rows_share, 0).astype(jnp.float32)
    grad_resid_rows = (out_rows + norm_back(resid_f, resid_scale, norm_rows)).astype(jnp.bfloat16)
    grad_block, enc_full, ffn_part = lax.optimization_barrier(
        (copies_to(grad_resid_rows, EIGHT), enc_full, ffn_part)
    )
    grad_other = pair_swap(grad_block)
    grad_mix = contract_last(grad_block, output_heads).astype(jnp.bfloat16)
    mix_heads_grad = (
        grad_mix.reshape(2, BLOCK, 2, HD).transpose(2, 0, 1, 3).reshape(4, BLOCK, HD)
    )
    grad_probs = jnp.einsum(
        "hqd,hkd->hqk", mix_heads_grad, value_heads, preferred_element_type=jnp.float32
    )
    row_dot = jnp.einsum(
        "hqd,hqd->hq", mix_heads_grad, head_mix, preferred_element_type=jnp.float32
    )[..., None]
    grad_scores = (attention * (grad_probs - row_dot) * score_factor).astype(jnp.bfloat16)
    grad_query = jnp.einsum(
        "hqk,hkd->hqd", grad_scores, key_heads, preferred_element_type=jnp.float32
    ).astype(jnp.bfloat16)
    grad_keys = jnp.einsum(
        "hqk,hqd->hkd", grad_scores, query_heads, preferred_element_type=jnp.float32
    ).astype(jnp.bfloat16)
    grad_values = jnp.einsum(
        "hqk,hqd->hkd", attention_b, mix_heads_grad, preferred_element_type=jnp.float32
    ).astype(jnp.bfloat16)
    head_grads = jnp.concatenate([grad_keys, grad_values, grad_query, head_mix], axis=1)
    head_grads, grad_other = lax.optimization_barrier((head_grads, grad_other))
    head_grads = head_grads.reshape((2, 2) + head_grads.shape[1:])
    own_grads = of_class(head_grads, 0, pair_place)
    other_grads = pair_swap(of_class(head_grads, 0, 1 - pair_place))
    query_from = 2 * keys_here
    mix_from = query_from + BLOCK
    swapped = in_pair_order(own_grads[:, :mix_from], other_grads[:, :mix_from], 1)
    both_grads = jnp.concatenate(
        [
            swapped[:, :, :keys_here].reshape(enc_columns, HD),
            swapped[:, :, keys_here:query_from].reshape(enc_columns, HD),
        ],
        axis=1,
    )
    query_grads = swapped[:, :, query_from:].reshape(token_count, HD)
    mix_own = own_grads[:, mix_from:].reshape(2 * BLOCK, HD)
    mix_other = other_grads[:, mix_from:].reshape(2 * BLOCK, HD)
    given, kept = weight_grads(
        enc_full, normed, grad_block, grad_other, both_grads, query_grads, mix_own, mix_other
    )
    given, kept, ffn_rows_sum = lax.optimization_barrier(
        (given, kept, scatter_sum(ffn_part, PLANE))
    )
    summed, query_grads = data_sum(given, kept, query_grads)
    summed = summed.astype(jnp.float32)
    query_grad = summed[:, :HD]
    key_grad = summed[:, HD : 2 * HD]
    value_grad = summed[:, 2 * HD : 3 * HD]
    mix_grad = summed[:, 3 * HD :].T
    layer_out = (resid_f + ffn_rows_sum).astype(jnp.bfloat16)
    input_part = contract_last(query_grads, query_weight)
    input_rows, query_grad, key_grad, value_grad, mix_grad = lax.optimization_barrier(
        (scatter_sum(input_part, PLANE), query_grad, key_grad, value_grad, mix_grad)
    )
    grad_tokens = (
        grad_resid_rows.astype(jnp.float32) + norm_back(token_rows, base_rows, input_rows)
    ).astype(jnp.bfloat16)
    return (layer_out, grad_tokens, query_grad, key_grad, value_grad, mix_grad)


def solution(mesh):
    mesh = jax.sharding.Mesh(
        mesh.devices.reshape(-1, 2, 2, 2, SIDE), DATA + PLANE
    )
    in_specs = (
        P(DATA, None),
        P(DATA, None, PLANE),
        P(DATA, None),
        P(DATA, None),
        P(None, PLANE),
        P(None, PLANE),
        P(None, PLANE),
        P(PLANE, None),
        P(DATA, PLANE),
        P(PLANE, DATA),
        P(DATA, None),
    )
    out_specs = (
        P(DATA + PLANE, None),
        P(DATA + PLANE, None),
        P(DATA, PLANE),
        P(DATA, PLANE),
        P(DATA, PLANE),
        P(PLANE, DATA),
    )
    return jax.shard_map(local, mesh=mesh, in_specs=in_specs, out_specs=out_specs, check_vma=False)
```

```python
import math

import jax
import jax.numpy as jnp
from jax import lax
from jax.experimental import pallas as pl
from jax.experimental.pallas import tpu as pltpu
from jax.sharding import PartitionSpec as P

HD = 128
BLOCK = 64
NLEN = 128
SIDE = 4
DATA = ("z", "core")
PLANE = ("yh", "yl", "x")
EIGHT = ("yh", "x")


epsilon = 1e-06
gelu_root = 0.7978845608028654
gelu_cubic = 0.044715


def rms_scale(values):
    return lax.rsqrt(jnp.mean(values * values, axis=-1, keepdims=True) + epsilon)


def norm_back(values, factor, incoming):
    normal_part = values * factor
    return (
        incoming - normal_part * jnp.mean(incoming * normal_part, axis=-1, keepdims=True)
    ) * factor


def gelu_value(inputs):
    inner = gelu_root * (inputs + gelu_cubic * inputs * inputs * inputs)
    return 0.5 * inputs * (1.0 + jnp.tanh(inner))


def gelu_slope(inputs):
    inner = gelu_root * (inputs + gelu_cubic * inputs * inputs * inputs)
    tanh_part = jnp.tanh(inner)
    return 0.5 * (1.0 + tanh_part) + 0.5 * inputs * (1.0 - tanh_part * tanh_part) * gelu_root * (
        1.0 + 3.0 * gelu_cubic * inputs * inputs
    )


def rounded(partial_value):
    return lax.optimization_barrier(partial_value.astype(jnp.bfloat16)).astype(jnp.float32)


def contract_last(left_side, right_side):
    return lax.dot_general(
        left_side, right_side, (((1,), (1,)), ((), ())), preferred_element_type=jnp.float32
    )


def contract_first(left_side, right_side):
    return lax.dot_general(
        left_side, right_side, (((0,), (0,)), ((), ())), preferred_element_type=jnp.float32
    )


def copies_to(rows, axis):
    size = lax.axis_size(axis)
    copies = jnp.broadcast_to(rows[None], (size,) + rows.shape)
    gathered = lax.all_to_all(copies, axis, split_axis=0, concat_axis=0, tiled=True)
    return gathered.reshape(size * rows.shape[0], rows.shape[1])


def scatter_sum(partial_rows, axis):
    size = lax.axis_size(axis)
    share = partial_rows.shape[0] // size
    swapped = lax.all_to_all(
        partial_rows.astype(jnp.bfloat16).reshape(size, share, partial_rows.shape[1]),
        axis,
        split_axis=0,
        concat_axis=0,
        tiled=True,
    )
    return jnp.sum(swapped.astype(jnp.float32), axis=0)


def in_pair_order(own, other, axis):
    first = lax.axis_index("yl") == 0
    return jnp.where(first, jnp.stack([own, other], axis), jnp.stack([other, own], axis))


def pair_swap(given):
    return lax.ppermute(given, "yl", [(0, 1), (1, 0)])


def weight_grads_kernel(
    core, enc, normed, grad_own, grad_other, both_grads, query_grads, mix_own, mix_other, given, kept
):
    step = pl.program_id(0)

    def times(left, right):
        return jnp.dot(left, right, preferred_element_type=jnp.float32)

    turned = jnp.concatenate(
        [
            times(query_grads[...], normed[...]),
            times(both_grads[...], enc[0]),
            times(mix_own[...], grad_own[...]) + times(mix_other[...], grad_other[...]),
        ],
        axis=0,
    )
    rows = turned.T.astype(jnp.bfloat16)
    mine = lax.rem(step, 2) == core[0]

    @pl.when(mine)
    def _():
        kept[0] = rows

    @pl.when(jnp.logical_not(mine))
    def _():
        given[0] = rows


def weight_grads(enc, normed, grad_own, grad_other, both_grads, query_grads, mix_own, mix_other):
    blocks, enc_rows, features = enc.shape
    token_count = normed.shape[0]
    columns = both_grads.shape[0] + query_grads.shape[0] + mix_own.shape[0]
    out_spec = pl.BlockSpec((1, features, columns), lambda step, core: (step // 2, 0, 0))
    out_shape = jax.ShapeDtypeStruct((blocks // 2, features, columns), jnp.bfloat16)
    small = [both_grads, query_grads, mix_own, mix_other]
    return pl.pallas_call(
        weight_grads_kernel,
        grid_spec=pltpu.PrefetchScalarGridSpec(
            num_scalar_prefetch=1,
            grid=(blocks,),
            in_specs=[
                pl.BlockSpec((1, enc_rows, features), lambda step, core: (step, 0, 0)),
                pl.BlockSpec((token_count, features), lambda step, core: (0, step)),
                pl.BlockSpec((grad_own.shape[0], features), lambda step, core: (0, step)),
                pl.BlockSpec((grad_own.shape[0], features), lambda step, core: (0, step)),
            ]
            + [pl.BlockSpec(part.shape, lambda step, core: (0, 0)) for part in small],
            out_specs=[out_spec, out_spec],
        ),
        out_shape=[out_shape, out_shape],
        cost_estimate=pl.CostEstimate(
            flops=2 * blocks * features * (enc_rows * 2 + token_count * 2) * HD,
            bytes_accessed=2 * blocks * features * (enc_rows + 2 * token_count + columns),
            transcendentals=0,
        ),
        compiler_params=pltpu.CompilerParams(vmem_limit_bytes=24 * 1024 * 1024),
    )(
        lax.axis_index("core").astype(jnp.int32).reshape(1),
        enc,
        normed,
        grad_own,
        grad_other,
        *small,
    )


def project_kernel(enc, first_weights, second_weights, out, total):
    step = pl.program_id(0)

    @pl.when(step == 0)
    def _():
        total[...] = jnp.zeros_like(total)

    total[0] += jnp.dot(enc[0], first_weights[...], preferred_element_type=jnp.float32)
    total[1] += jnp.dot(enc[0], second_weights[...], preferred_element_type=jnp.float32)

    @pl.when(step == pl.num_programs(0) - 1)
    def _():
        out[...] = total[...].astype(out.dtype)


def project(enc, first_weights, second_weights):
    blocks, rows, features = enc.shape
    columns = first_weights.shape[1]
    weight_spec = pl.BlockSpec((features, columns), lambda step: (step, 0))
    return pl.pallas_call(
        project_kernel,
        grid=(blocks,),
        in_specs=[
            pl.BlockSpec((1, rows, features), lambda step: (step, 0, 0)),
            weight_spec,
            weight_spec,
        ],
        out_specs=pl.BlockSpec((2, rows, columns), lambda step: (0, 0, 0)),
        out_shape=jax.ShapeDtypeStruct((2, rows, columns), jnp.bfloat16),
        scratch_shapes=[pltpu.VMEM((2, rows, columns), jnp.float32)],
        cost_estimate=pl.CostEstimate(
            flops=4 * blocks * features * rows * columns,
            bytes_accessed=2 * blocks * features * (rows + 2 * columns),
            transcendentals=0,
        ),
        compiler_params=pltpu.CompilerParams(vmem_limit_bytes=24 * 1024 * 1024),
    )(enc, first_weights, second_weights)


def data_sum(given, kept, after):
    got = lax.ppermute(given, "core", [(0, 1), (1, 0)])
    paired = (kept.astype(jnp.float32) + got.astype(jnp.float32)).astype(jnp.bfloat16)
    paired, after = lax.optimization_barrier((paired, after))
    summed = lax.psum_scatter(paired, "z", scatter_dimension=0, tiled=False)
    return summed, after


def local(
    tokens,
    neighbour_buffer,
    shard_ids,
    row_ids,
    query_weight,
    key_weight,
    value_weight,
    output_weight,
    up_weight,
    down_weight,
    grad_output,
):
    data_size = lax.axis_size(DATA)
    tensor_size = lax.axis_size(PLANE)
    token_count = tokens.shape[0]
    width = tokens.shape[1]
    block_count = shard_ids.shape[0]
    capacity = block_count // 2
    pair_count = 2 * block_count
    owners = shard_ids.reshape(pair_count)
    wanted = row_ids.reshape(pair_count)
    same_owner = owners[:, None] == owners[None, :]
    earlier = lax.broadcasted_iota(jnp.int32, (pair_count, pair_count), 0) < lax.broadcasted_iota(
        jnp.int32, (pair_count, pair_count), 1
    )
    slot_index = jnp.sum((same_owner & earlier).astype(jnp.int32), axis=0)
    owner_grid = lax.broadcasted_iota(jnp.int32, (data_size, capacity, pair_count), 0)
    slot_grid = lax.broadcasted_iota(jnp.int32, (data_size, capacity, pair_count), 1)
    slot_match = (owners[None, None, :] == owner_grid) & (slot_index[None, None, :] == slot_grid)
    requests = jnp.sum(jnp.where(slot_match, wanted[None, None, :], 0), axis=2)
    asked = lax.all_to_all(requests, DATA, split_axis=0, concat_axis=0, tiled=True)
    replies = lax.all_to_all(
        jnp.take(neighbour_buffer, asked, axis=0, mode="clip"),
        DATA,
        split_axis=0,
        concat_axis=0,
        tiled=True,
    )
    reply_rows = replies.reshape((data_size * capacity,) + replies.shape[2:])
    mine = jnp.take(reply_rows, owners * capacity + slot_index, axis=0, mode="clip")
    enc_mine = mine.reshape(pair_count * NLEN, -1)
    both_weights = jnp.concatenate([key_weight, value_weight], axis=1)
    pair_weights = pair_swap(both_weights)
    pair_output = pair_swap(output_weight)
    pair_place = lax.axis_index("yl")
    token_f = tokens.astype(jnp.float32)
    base_scale = rms_scale(token_f)
    normed = (token_f * base_scale).astype(jnp.bfloat16)
    query_rows = jnp.dot(normed, query_weight, preferred_element_type=jnp.float32).astype(
        jnp.bfloat16
    )
    query_blocks = query_rows.reshape(2, 2, BLOCK, HD)

    def of_class(blocks, axis, place):
        return lax.dynamic_index_in_dim(blocks, place, axis, keepdims=False)

    query_heads = jnp.stack(
        [
            of_class(query_blocks, 1, pair_place),
            pair_swap(of_class(query_blocks, 1, 1 - pair_place)),
        ]
    )
    frozen = jnp.concatenate([up_weight, down_weight.T], axis=1)
    enc_mine, query_heads, frozen, pair_weights, pair_output = lax.optimization_barrier(
        (enc_mine, query_heads, frozen, pair_weights, pair_output)
    )
    output_heads = jnp.concatenate([output_weight, pair_output], axis=0)
    enc_columns, features = enc_mine.shape
    keys_here = 2 * NLEN
    class_pieces = jnp.swapaxes(enc_mine.reshape(2, 2, keys_here, features), 0, 1)
    enc_block = lax.all_to_all(
        jnp.broadcast_to(
            class_pieces.reshape(1, 2, 1, 2 * keys_here, features),
            (2, 2, SIDE, 2 * keys_here, features),
        ).reshape(tensor_size, 2 * keys_here, features),
        PLANE,
        split_axis=0,
        concat_axis=0,
        tiled=True,
    )
    enc_block, output_heads, enc_mine = lax.optimization_barrier(
        (enc_block, output_heads, enc_mine)
    )
    frozen_full = lax.all_gather(frozen, DATA, axis=0, tiled=True)
    hidden = up_weight.shape[1]
    up_full = frozen_full[:, :hidden]
    down_turned = frozen_full[:, hidden:]
    both_heads = project(enc_block, both_weights, pair_weights).reshape(4, keys_here, 2 * HD)
    query_heads = query_heads.reshape(4, BLOCK, HD)
    key_heads = both_heads[:, :, :HD]
    value_heads = both_heads[:, :, HD:]
    score_factor = 1.0 / math.sqrt(HD)
    scores = (
        jnp.einsum("hqd,hkd->hqk", query_heads, key_heads, preferred_element_type=jnp.float32)
        * score_factor
    )
    raised = jnp.exp(scores)
    attention = raised / jnp.sum(raised, axis=-1, keepdims=True)
    attention_b = attention.astype(jnp.bfloat16)
    head_mix = jnp.einsum(
        "hqk,hkd->hqd", attention_b, value_heads, preferred_element_type=jnp.float32
    ).astype(jnp.bfloat16)
    mix_rows = head_mix.reshape(2, 2, BLOCK, HD).transpose(1, 2, 0, 3).reshape(2 * BLOCK, 2 * HD)
    attn_part = jnp.dot(mix_rows, output_heads, preferred_element_type=jnp.float32)
    rows_share = token_count // tensor_size
    row_start = lax.axis_index(PLANE) * rows_share
    token_rows = lax.dynamic_slice_in_dim(tokens, row_start, rows_share, 0).astype(jnp.float32)
    base_rows = lax.dynamic_slice_in_dim(base_scale, row_start, rows_share, 0)
    attn_rows, enc_mine = lax.optimization_barrier((scatter_sum(attn_part, EIGHT), enc_mine))
    enc_full = lax.all_gather(enc_mine, PLANE, axis=0, tiled=False)
    resid_f = rounded(token_rows + attn_rows)
    resid_scale = rms_scale(resid_f)
    ffn_in = copies_to((resid_f * resid_scale).astype(jnp.bfloat16), PLANE)
    grad_act = lax.optimization_barrier(
        jnp.dot(grad_output, down_turned, preferred_element_type=jnp.float32)
    )
    pre_act = jnp.dot(ffn_in, up_full, preferred_element_type=jnp.float32)
    activated = gelu_value(pre_act).astype(jnp.bfloat16)
    grad_pre = (grad_act * gelu_slope(pre_act)).astype(jnp.bfloat16)
    norm_part = contract_last(grad_pre, up_full)
    ffn_part = contract_last(activated, down_turned).astype(jnp.bfloat16)
    norm_rows = scatter_sum(norm_part, PLANE)
    out_rows = lax.dynamic_slice_in_dim(grad_output, row_start, rows_share, 0).astype(jnp.float32)
    grad_resid_rows = (out_rows + norm_back(resid_f, resid_scale, norm_rows)).astype(jnp.bfloat16)
    grad_block, enc_full, ffn_part = lax.optimization_barrier(
        (copies_to(grad_resid_rows, EIGHT), enc_full, ffn_part)
    )
    grad_other = pair_swap(grad_block)
    grad_mix = contract_last(grad_block, output_heads).astype(jnp.bfloat16)
    mix_heads_grad = (
        grad_mix.reshape(2, BLOCK, 2, HD).transpose(2, 0, 1, 3).reshape(4, BLOCK, HD)
    )
    grad_probs = jnp.einsum(
        "hqd,hkd->hqk", mix_heads_grad, value_heads, preferred_element_type=jnp.float32
    )
    row_dot = jnp.einsum(
        "hqd,hqd->hq", mix_heads_grad, head_mix, preferred_element_type=jnp.float32
    )[..., None]
    grad_scores = (attention * (grad_probs - row_dot) * score_factor).astype(jnp.bfloat16)
    grad_query = jnp.einsum(
        "hqk,hkd->hqd", grad_scores, key_heads, preferred_element_type=jnp.float32
    ).astype(jnp.bfloat16)
    grad_keys = jnp.einsum(
        "hqk,hqd->hkd", grad_scores, query_heads, preferred_element_type=jnp.float32
    ).astype(jnp.bfloat16)
    grad_values = jnp.einsum(
        "hqk,hqd->hkd", attention_b, mix_heads_grad, preferred_element_type=jnp.float32
    ).astype(jnp.bfloat16)
    head_grads = jnp.concatenate([grad_keys, grad_values, grad_query, head_mix], axis=1)
    head_grads, grad_other, ffn_part = lax.optimization_barrier(
        (head_grads, grad_other, ffn_part)
    )
    ffn_rows_sum = scatter_sum(ffn_part, PLANE)
    head_grads = head_grads.reshape((2, 2) + head_grads.shape[1:])
    own_grads = head_grads[0]
    other_grads = pair_swap(head_grads[1])
    query_from = 2 * keys_here
    mix_from = query_from + BLOCK
    swapped = in_pair_order(own_grads[:, :mix_from], other_grads[:, :mix_from], 1)
    both_grads = jnp.concatenate(
        [
            swapped[:, :, :keys_here].reshape(enc_columns, HD),
            swapped[:, :, keys_here:query_from].reshape(enc_columns, HD),
        ],
        axis=1,
    )
    query_grads = swapped[:, :, query_from:].reshape(token_count, HD)
    mix_own = own_grads[:, mix_from:].reshape(2 * BLOCK, HD)
    mix_other = other_grads[:, mix_from:].reshape(2 * BLOCK, HD)
    given, kept = weight_grads(
        enc_full,
        normed,
        grad_block,
        grad_other,
        both_grads.T,
        query_grads.T,
        mix_own.T,
        mix_other.T,
    )
    given, kept, ffn_rows_sum = lax.optimization_barrier((given, kept, ffn_rows_sum))
    summed, query_grads = data_sum(given, kept, query_grads)
    summed = summed.astype(jnp.float32)
    query_grad = summed[:, :HD]
    key_grad = summed[:, HD : 2 * HD]
    value_grad = summed[:, 2 * HD : 3 * HD]
    mix_grad = summed[:, 3 * HD :].T
    layer_out = (resid_f + ffn_rows_sum).astype(jnp.bfloat16)
    input_part = contract_last(query_grads, query_weight)
    input_rows, query_grad, key_grad, value_grad, mix_grad = lax.optimization_barrier(
        (scatter_sum(input_part, PLANE), query_grad, key_grad, value_grad, mix_grad)
    )
    grad_tokens = (
        grad_resid_rows.astype(jnp.float32) + norm_back(token_rows, base_rows, input_rows)
    ).astype(jnp.bfloat16)
    return (layer_out, grad_tokens, query_grad, key_grad, value_grad, mix_grad)


def solution(mesh):
    mesh = jax.sharding.Mesh(
        mesh.devices.reshape(-1, 2, 2, 2, SIDE), DATA + PLANE
    )
    in_specs = (
        P(DATA, None),
        P(DATA, None, PLANE),
        P(DATA, None),
        P(DATA, None),
        P(None, PLANE),
        P(None, PLANE),
        P(None, PLANE),
        P(PLANE, None),
        P(DATA, PLANE),
        P(PLANE, DATA),
        P(DATA, None),
    )
    out_specs = (
        P(DATA + PLANE, None),
        P(DATA + PLANE, None),
        P(DATA, PLANE),
        P(DATA, PLANE),
        P(DATA, PLANE),
        P(PLANE, DATA),
    )
    return jax.shard_map(local, mesh=mesh, in_specs=in_specs, out_specs=out_specs, check_vma=False)
```

```python
import math

import jax
import jax.numpy as jnp
from jax import lax
from jax.sharding import PartitionSpec as P

HD = 128
BLOCK = 64
NLEN = 128
SIDE = 4
DATA = ("z", "core")
PLANE = ("y", "x")


epsilon = 1e-06
gelu_root = 0.7978845608028654
gelu_cubic = 0.044715


def rms_scale(values):
    return lax.rsqrt(jnp.mean(values * values, axis=-1, keepdims=True) + epsilon)


def norm_back(values, factor, incoming):
    normal_part = values * factor
    return (
        incoming - normal_part * jnp.mean(incoming * normal_part, axis=-1, keepdims=True)
    ) * factor


def gelu_value(inputs):
    inner = gelu_root * (inputs + gelu_cubic * inputs * inputs * inputs)
    return 0.5 * inputs * (1.0 + jnp.tanh(inner))


def gelu_slope(inputs):
    inner = gelu_root * (inputs + gelu_cubic * inputs * inputs * inputs)
    tanh_part = jnp.tanh(inner)
    return 0.5 * (1.0 + tanh_part) + 0.5 * inputs * (1.0 - tanh_part * tanh_part) * gelu_root * (
        1.0 + 3.0 * gelu_cubic * inputs * inputs
    )


def rounded(partial_value):
    return lax.optimization_barrier(partial_value.astype(jnp.bfloat16)).astype(jnp.float32)


def contract_last(left_side, right_side):
    return lax.dot_general(
        left_side, right_side, (((1,), (1,)), ((), ())), preferred_element_type=jnp.float32
    )


def contract_first(left_side, right_side):
    return lax.dot_general(
        left_side, right_side, (((0,), (0,)), ((), ())), preferred_element_type=jnp.float32
    )


def ring_shift(piece, axis, step):
    return lax.ppermute(
        piece, axis, [(place, (place + step) % SIDE) for place in range(SIDE)]
    )


def ring_gather(piece, axis, split_axis):
    here = lax.axis_index(axis)
    from_prev = ring_shift(piece, axis, 1)
    from_next = ring_shift(piece, axis, -1)
    half = piece.shape[split_axis] // 2
    first = lax.slice_in_dim(from_prev, 0, half, axis=split_axis)
    second = lax.slice_in_dim(from_next, half, 2 * half, axis=split_axis)
    opposite = jnp.concatenate(
        [ring_shift(first, axis, 1), ring_shift(second, axis, -1)], axis=split_axis
    )
    stacked = jnp.zeros((SIDE,) + piece.shape, piece.dtype)
    for shift, part in ((0, piece), (-1, from_prev), (1, from_next), (2, opposite)):
        stacked = lax.dynamic_update_index_in_dim(
            stacked, part, lax.rem(here + shift + SIDE, SIDE), 0
        )
    return stacked


def plane_gather(piece, halve_axis, split_axis):
    half = piece.shape[halve_axis] // 2
    first = lax.slice_in_dim(piece, 0, half, axis=halve_axis)
    second = lax.slice_in_dim(piece, half, 2 * half, axis=halve_axis)
    first = ring_gather(first, "x", split_axis)
    second = ring_gather(second, "y", split_axis)
    first = ring_gather(first, "y", split_axis + 1)
    second = ring_gather(second, "x", split_axis + 1)
    return first, jnp.swapaxes(second, 0, 1)


def gather_rows(rows):
    first, second = plane_gather(rows, 1, 1)
    count = SIDE * SIDE * rows.shape[0]
    half = rows.shape[1] // 2
    return jnp.concatenate([first.reshape(count, half), second.reshape(count, half)], axis=1)


def copies_to(rows, axis):
    size = lax.axis_size(axis)
    copies = jnp.broadcast_to(rows[None], (size,) + rows.shape)
    gathered = lax.all_to_all(copies, axis, split_axis=0, concat_axis=0, tiled=True)
    return gathered.reshape(size * rows.shape[0], rows.shape[1])


def scatter_sum(partial_rows, axis):
    size = lax.axis_size(axis)
    share = partial_rows.shape[0] // size
    swapped = lax.all_to_all(
        partial_rows.astype(jnp.bfloat16).reshape(size, share, partial_rows.shape[1]),
        axis,
        split_axis=0,
        concat_axis=0,
        tiled=True,
    )
    return jnp.sum(swapped.astype(jnp.float32), axis=0)


def data_sum(partial_rows, after):
    core = lax.axis_index("core")
    shares = partial_rows.reshape(lax.axis_size("z"), 2, -1, partial_rows.shape[1])
    given = lax.dynamic_index_in_dim(shares, 1 - core, 1, keepdims=False)
    kept = lax.dynamic_index_in_dim(shares, core, 1, keepdims=False)
    got = lax.ppermute(given, "core", [(0, 1), (1, 0)])
    paired = (kept.astype(jnp.float32) + got.astype(jnp.float32)).astype(jnp.bfloat16)
    paired, after = lax.optimization_barrier((paired, after))
    summed = lax.psum_scatter(paired, "z", scatter_dimension=0, tiled=False)
    return summed, after


def local(
    tokens,
    neighbour_buffer,
    shard_ids,
    row_ids,
    query_weight,
    key_weight,
    value_weight,
    output_weight,
    up_weight,
    down_weight,
    grad_output,
):
    data_size = lax.axis_size(DATA)
    tensor_size = lax.axis_size(PLANE)
    token_count = tokens.shape[0]
    width = tokens.shape[1]
    block_count = shard_ids.shape[0]
    capacity = block_count // 2
    pair_count = 2 * block_count
    owners = shard_ids.reshape(pair_count)
    wanted = row_ids.reshape(pair_count)
    same_owner = owners[:, None] == owners[None, :]
    earlier = lax.broadcasted_iota(jnp.int32, (pair_count, pair_count), 0) < lax.broadcasted_iota(
        jnp.int32, (pair_count, pair_count), 1
    )
    slot_index = jnp.sum((same_owner & earlier).astype(jnp.int32), axis=0)
    owner_grid = lax.broadcasted_iota(jnp.int32, (data_size, capacity, pair_count), 0)
    slot_grid = lax.broadcasted_iota(jnp.int32, (data_size, capacity, pair_count), 1)
    slot_match = (owners[None, None, :] == owner_grid) & (slot_index[None, None, :] == slot_grid)
    requests = jnp.sum(jnp.where(slot_match, wanted[None, None, :], 0), axis=2)
    asked = lax.all_to_all(requests, DATA, split_axis=0, concat_axis=0, tiled=True)
    replies = lax.all_to_all(
        jnp.take(neighbour_buffer, asked, axis=0, mode="clip"),
        DATA,
        split_axis=0,
        concat_axis=0,
        tiled=True,
    )
    reply_rows = replies.reshape(data_size * capacity, replies.shape[2], replies.shape[3])
    local_enc = jnp.take(reply_rows, owners * capacity + slot_index, axis=0, mode="clip")
    frozen = jnp.concatenate([up_weight, down_weight.T], axis=1)
    local_enc, frozen = lax.optimization_barrier((local_enc, frozen))
    frozen_full = lax.all_gather(frozen, DATA, axis=0, tiled=True)
    hidden = up_weight.shape[1]
    up_full = frozen_full[:, :hidden]
    down_turned = frozen_full[:, hidden:]
    enc_a, enc_b = plane_gather(local_enc.reshape(pair_count * NLEN, width // tensor_size), 0, 0)
    half_rows = pair_count * NLEN // 2
    enc_rows = jnp.concatenate(
        [
            enc_a.transpose(2, 0, 1, 3).reshape(half_rows, width),
            enc_b.transpose(2, 0, 1, 3).reshape(half_rows, width),
        ],
        axis=0,
    )
    token_f = tokens.astype(jnp.float32)
    base_scale = rms_scale(token_f)
    normed = (token_f * base_scale).astype(jnp.bfloat16)
    query_rows = jnp.dot(normed, query_weight, preferred_element_type=jnp.float32).astype(
        jnp.bfloat16
    )
    head_width = query_rows.shape[1]
    both_weights = jnp.concatenate([key_weight, value_weight], axis=1)
    both_rows = jnp.dot(enc_rows, both_weights, preferred_element_type=jnp.float32).astype(
        jnp.bfloat16
    )
    key_rows = both_rows[:, :head_width]
    value_rows = both_rows[:, head_width:]
    heads_here = head_width // HD
    query_heads = query_rows.reshape(block_count, BLOCK, heads_here, HD)
    key_heads = key_rows.reshape(block_count, 2 * NLEN, heads_here, HD)
    value_heads = value_rows.reshape(block_count, 2 * NLEN, heads_here, HD)
    score_factor = 1.0 / math.sqrt(HD)
    scores = (
        jnp.einsum("cqhd,ckhd->chqk", query_heads, key_heads, preferred_element_type=jnp.float32)
        * score_factor
    )
    raised = jnp.exp(scores)
    attention = raised / jnp.sum(raised, axis=-1, keepdims=True)
    attention_b = attention.astype(jnp.bfloat16)
    head_mix = jnp.einsum(
        "chqk,ckhd->cqhd", attention_b, value_heads, preferred_element_type=jnp.float32
    ).astype(jnp.bfloat16)
    mix_rows = head_mix.reshape(token_count, head_width)
    attn_part = jnp.dot(mix_rows, output_weight, preferred_element_type=jnp.float32)
    rows_share = token_count // tensor_size
    row_start = lax.axis_index(PLANE) * rows_share
    token_rows = lax.dynamic_slice_in_dim(token_f, row_start, rows_share, 0)
    base_rows = lax.dynamic_slice_in_dim(base_scale, row_start, rows_share, 0)
    attn_rows = scatter_sum(attn_part, PLANE)
    resid_f = rounded(token_rows + attn_rows)
    resid_scale = rms_scale(resid_f)
    ffn_in = copies_to((resid_f * resid_scale).astype(jnp.bfloat16), PLANE)
    grad_act = lax.optimization_barrier(
        jnp.dot(grad_output, down_turned, preferred_element_type=jnp.float32)
    )
    pre_act = jnp.dot(ffn_in, up_full, preferred_element_type=jnp.float32)
    activated = gelu_value(pre_act).astype(jnp.bfloat16)
    grad_pre = (grad_act * gelu_slope(pre_act)).astype(jnp.bfloat16)
    norm_part = contract_last(grad_pre, up_full)
    ffn_part = contract_last(activated, down_turned).astype(jnp.bfloat16)
    norm_rows = scatter_sum(norm_part, PLANE)
    out_rows = lax.dynamic_slice_in_dim(grad_output, row_start, rows_share, 0).astype(jnp.float32)
    grad_resid_rows = (out_rows + norm_back(resid_f, resid_scale, norm_rows)).astype(jnp.bfloat16)
    grad_resid, ffn_part = lax.optimization_barrier((gather_rows(grad_resid_rows), ffn_part))
    grad_mix = contract_last(grad_resid, output_weight).astype(jnp.bfloat16)
    mix_heads_grad = grad_mix.reshape(block_count, BLOCK, heads_here, HD)
    grad_probs = jnp.einsum(
        "cqhd,ckhd->chqk", mix_heads_grad, value_heads, preferred_element_type=jnp.float32
    )
    row_dot = jnp.einsum(
        "cqhd,cqhd->chq", mix_heads_grad, head_mix, preferred_element_type=jnp.float32
    )[..., None]
    grad_scores = (attention * (grad_probs - row_dot) * score_factor).astype(jnp.bfloat16)
    grad_query = (
        jnp.einsum("chqk,ckhd->cqhd", grad_scores, key_heads, preferred_element_type=jnp.float32)
        .astype(jnp.bfloat16)
        .reshape(token_count, head_width)
    )
    grad_keys = (
        jnp.einsum("chqk,cqhd->ckhd", grad_scores, query_heads, preferred_element_type=jnp.float32)
        .astype(jnp.bfloat16)
        .reshape(pair_count * NLEN, head_width)
    )
    grad_values = (
        jnp.einsum(
            "chqk,cqhd->ckhd", attention_b, mix_heads_grad, preferred_element_type=jnp.float32
        )
        .astype(jnp.bfloat16)
        .reshape(pair_count * NLEN, head_width)
    )
    weight_parts = jnp.concatenate(
        [
            contract_first(normed, grad_query),
            contract_first(enc_rows, jnp.concatenate([grad_keys, grad_values], axis=1)),
            contract_first(grad_resid, mix_rows),
        ],
        axis=1,
    ).astype(jnp.bfloat16)
    weight_parts, ffn_rows_sum = lax.optimization_barrier(
        (weight_parts, scatter_sum(ffn_part, PLANE))
    )
    summed, grad_query = data_sum(weight_parts, grad_query)
    summed = summed.astype(jnp.float32)
    query_grad = summed[:, :HD]
    key_grad = summed[:, HD : 2 * HD]
    value_grad = summed[:, 2 * HD : 3 * HD]
    mix_grad = summed[:, 3 * HD :].T
    layer_out = (resid_f + ffn_rows_sum).astype(jnp.bfloat16)
    input_part = contract_last(grad_query, query_weight)
    input_rows = scatter_sum(input_part, PLANE)
    grad_tokens = (
        grad_resid_rows.astype(jnp.float32) + norm_back(token_rows, base_rows, input_rows)
    ).astype(jnp.bfloat16)
    return (layer_out, grad_tokens, query_grad, key_grad, value_grad, mix_grad)


def solution(mesh):
    mesh = jax.sharding.Mesh(
        mesh.devices.reshape(-1, 2, SIDE, SIDE), DATA + PLANE
    )
    in_specs = (
        P(DATA, None),
        P(DATA, None, PLANE),
        P(DATA, None),
        P(DATA, None),
        P(None, PLANE),
        P(None, PLANE),
        P(None, PLANE),
        P(PLANE, None),
        P(DATA, PLANE),
        P(PLANE, DATA),
        P(DATA, None),
    )
    out_specs = (
        P(DATA + PLANE, None),
        P(DATA + PLANE, None),
        P(DATA, PLANE),
        P(DATA, PLANE),
        P(DATA, PLANE),
        P(PLANE, DATA),
    )
    return jax.shard_map(local, mesh=mesh, in_specs=in_specs, out_specs=out_specs, check_vma=False)
```

```python
import math

import jax
import jax.numpy as jnp
from jax import lax
from jax.sharding import PartitionSpec as P

HD = 128
BLOCK = 64
NLEN = 128
SIDE = 4
DATA = ("z", "core")
PLANE = ("y", "x")


epsilon = 1e-06
gelu_root = 0.7978845608028654
gelu_cubic = 0.044715


def rms_scale(values):
    return lax.rsqrt(jnp.mean(values * values, axis=-1, keepdims=True) + epsilon)


def norm_back(values, factor, incoming):
    normal_part = values * factor
    return (
        incoming - normal_part * jnp.mean(incoming * normal_part, axis=-1, keepdims=True)
    ) * factor


def gelu_value(inputs):
    inner = gelu_root * (inputs + gelu_cubic * inputs * inputs * inputs)
    return 0.5 * inputs * (1.0 + jnp.tanh(inner))


def gelu_slope(inputs):
    inner = gelu_root * (inputs + gelu_cubic * inputs * inputs * inputs)
    tanh_part = jnp.tanh(inner)
    return 0.5 * (1.0 + tanh_part) + 0.5 * inputs * (1.0 - tanh_part * tanh_part) * gelu_root * (
        1.0 + 3.0 * gelu_cubic * inputs * inputs
    )


def rounded(partial_value):
    return lax.optimization_barrier(partial_value.astype(jnp.bfloat16)).astype(jnp.float32)


def contract_last(left_side, right_side):
    return lax.dot_general(
        left_side, right_side, (((1,), (1,)), ((), ())), preferred_element_type=jnp.float32
    )


def contract_first(left_side, right_side):
    return lax.dot_general(
        left_side, right_side, (((0,), (0,)), ((), ())), preferred_element_type=jnp.float32
    )


def ring_shift(piece, axis, step):
    return lax.ppermute(
        piece, axis, [(place, (place + step) % SIDE) for place in range(SIDE)]
    )


def ring_gather(piece, axis, split_axis):
    here = lax.axis_index(axis)
    from_prev = ring_shift(piece, axis, 1)
    from_next = ring_shift(piece, axis, -1)
    half = piece.shape[split_axis] // 2
    first = lax.slice_in_dim(from_prev, 0, half, axis=split_axis)
    second = lax.slice_in_dim(from_next, half, 2 * half, axis=split_axis)
    opposite = jnp.concatenate(
        [ring_shift(first, axis, 1), ring_shift(second, axis, -1)], axis=split_axis
    )
    stacked = jnp.zeros((SIDE,) + piece.shape, piece.dtype)
    for shift, part in ((0, piece), (-1, from_prev), (1, from_next), (2, opposite)):
        stacked = lax.dynamic_update_index_in_dim(
            stacked, part, lax.rem(here + shift + SIDE, SIDE), 0
        )
    return stacked


def plane_gather(piece, halve_axis, split_axis):
    half = piece.shape[halve_axis] // 2
    first = lax.slice_in_dim(piece, 0, half, axis=halve_axis)
    second = lax.slice_in_dim(piece, half, 2 * half, axis=halve_axis)
    first = ring_gather(first, "x", split_axis)
    second = ring_gather(second, "y", split_axis)
    first = ring_gather(first, "y", split_axis + 1)
    second = ring_gather(second, "x", split_axis + 1)
    return first, jnp.swapaxes(second, 0, 1)


def gather_rows(rows):
    first, second = plane_gather(rows, 1, 1)
    count = SIDE * SIDE * rows.shape[0]
    half = rows.shape[1] // 2
    return jnp.concatenate([first.reshape(count, half), second.reshape(count, half)], axis=1)


def copies_to(rows, axis):
    size = lax.axis_size(axis)
    copies = jnp.broadcast_to(rows[None], (size,) + rows.shape)
    gathered = lax.all_to_all(copies, axis, split_axis=0, concat_axis=0, tiled=True)
    return gathered.reshape(size * rows.shape[0], rows.shape[1])


def scatter_sum(partial_rows, axis):
    size = lax.axis_size(axis)
    share = partial_rows.shape[0] // size
    swapped = lax.all_to_all(
        partial_rows.astype(jnp.bfloat16).reshape(size, share, partial_rows.shape[1]),
        axis,
        split_axis=0,
        concat_axis=0,
        tiled=True,
    )
    return jnp.sum(swapped.astype(jnp.float32), axis=0)


def local(
    tokens,
    neighbour_buffer,
    shard_ids,
    row_ids,
    query_weight,
    key_weight,
    value_weight,
    output_weight,
    up_weight,
    down_weight,
    grad_output,
):
    data_size = lax.axis_size(DATA)
    tensor_size = lax.axis_size(PLANE)
    token_count = tokens.shape[0]
    width = tokens.shape[1]
    block_count = shard_ids.shape[0]
    capacity = block_count // 2
    pair_count = 2 * block_count
    owners = shard_ids.reshape(pair_count)
    wanted = row_ids.reshape(pair_count)
    same_owner = owners[:, None] == owners[None, :]
    earlier = lax.broadcasted_iota(jnp.int32, (pair_count, pair_count), 0) < lax.broadcasted_iota(
        jnp.int32, (pair_count, pair_count), 1
    )
    slot_index = jnp.sum((same_owner & earlier).astype(jnp.int32), axis=0)
    owner_grid = lax.broadcasted_iota(jnp.int32, (data_size, capacity, pair_count), 0)
    slot_grid = lax.broadcasted_iota(jnp.int32, (data_size, capacity, pair_count), 1)
    slot_match = (owners[None, None, :] == owner_grid) & (slot_index[None, None, :] == slot_grid)
    requests = jnp.sum(jnp.where(slot_match, wanted[None, None, :], 0), axis=2)
    asked = lax.all_to_all(requests, DATA, split_axis=0, concat_axis=0, tiled=True)
    replies = lax.all_to_all(
        jnp.take(neighbour_buffer, asked, axis=0, mode="clip"),
        DATA,
        split_axis=0,
        concat_axis=0,
        tiled=True,
    )
    reply_rows = replies.reshape(data_size * capacity, replies.shape[2], replies.shape[3])
    local_enc = jnp.take(reply_rows, owners * capacity + slot_index, axis=0, mode="clip")
    frozen = jnp.concatenate([up_weight, down_weight.T], axis=1)
    local_enc, frozen = lax.optimization_barrier((local_enc, frozen))
    frozen_full = lax.all_gather(frozen, DATA, axis=0, tiled=True)
    hidden = up_weight.shape[1]
    up_full = frozen_full[:, :hidden]
    down_turned = frozen_full[:, hidden:]
    enc_a, enc_b = plane_gather(local_enc.reshape(pair_count * NLEN, width // tensor_size), 0, 0)
    half_rows = pair_count * NLEN // 2
    enc_rows = jnp.concatenate(
        [
            enc_a.transpose(2, 0, 1, 3).reshape(half_rows, width),
            enc_b.transpose(2, 0, 1, 3).reshape(half_rows, width),
        ],
        axis=0,
    )
    token_f = tokens.astype(jnp.float32)
    base_scale = rms_scale(token_f)
    normed = (token_f * base_scale).astype(jnp.bfloat16)
    query_rows = jnp.dot(normed, query_weight, preferred_element_type=jnp.float32).astype(
        jnp.bfloat16
    )
    head_width = query_rows.shape[1]
    both_weights = jnp.concatenate([key_weight, value_weight], axis=1)
    both_rows = jnp.dot(enc_rows, both_weights, preferred_element_type=jnp.float32).astype(
        jnp.bfloat16
    )
    key_rows = both_rows[:, :head_width]
    value_rows = both_rows[:, head_width:]
    heads_here = head_width // HD
    query_heads = query_rows.reshape(block_count, BLOCK, heads_here, HD)
    key_heads = key_rows.reshape(block_count, 2 * NLEN, heads_here, HD)
    value_heads = value_rows.reshape(block_count, 2 * NLEN, heads_here, HD)
    score_factor = 1.0 / math.sqrt(HD)
    scores = (
        jnp.einsum("cqhd,ckhd->chqk", query_heads, key_heads, preferred_element_type=jnp.float32)
        * score_factor
    )
    raised = jnp.exp(scores)
    attention = raised / jnp.sum(raised, axis=-1, keepdims=True)
    attention_b = attention.astype(jnp.bfloat16)
    head_mix = jnp.einsum(
        "chqk,ckhd->cqhd", attention_b, value_heads, preferred_element_type=jnp.float32
    ).astype(jnp.bfloat16)
    mix_rows = head_mix.reshape(token_count, head_width)
    attn_part = jnp.dot(mix_rows, output_weight, preferred_element_type=jnp.float32)
    rows_share = token_count // tensor_size
    row_start = lax.axis_index(PLANE) * rows_share
    token_rows = lax.dynamic_slice_in_dim(token_f, row_start, rows_share, 0)
    base_rows = lax.dynamic_slice_in_dim(base_scale, row_start, rows_share, 0)
    attn_rows = scatter_sum(attn_part, PLANE)
    resid_f = rounded(token_rows + attn_rows)
    resid_scale = rms_scale(resid_f)
    ffn_in = copies_to((resid_f * resid_scale).astype(jnp.bfloat16), PLANE)
    grad_act = lax.optimization_barrier(
        jnp.dot(grad_output, down_turned, preferred_element_type=jnp.float32)
    )
    pre_act = jnp.dot(ffn_in, up_full, preferred_element_type=jnp.float32)
    activated = gelu_value(pre_act).astype(jnp.bfloat16)
    grad_pre = (grad_act * gelu_slope(pre_act)).astype(jnp.bfloat16)
    norm_part = contract_last(grad_pre, up_full)
    norm_rows = scatter_sum(norm_part, PLANE)
    out_rows = lax.dynamic_slice_in_dim(grad_output, row_start, rows_share, 0).astype(jnp.float32)
    grad_resid_rows = (out_rows + norm_back(resid_f, resid_scale, norm_rows)).astype(jnp.bfloat16)
    grad_resid = gather_rows(grad_resid_rows)
    grad_mix = contract_last(grad_resid, output_weight).astype(jnp.bfloat16)
    mix_heads_grad = grad_mix.reshape(block_count, BLOCK, heads_here, HD)
    grad_probs = jnp.einsum(
        "cqhd,ckhd->chqk", mix_heads_grad, value_heads, preferred_element_type=jnp.float32
    )
    row_dot = jnp.einsum(
        "cqhd,cqhd->chq", mix_heads_grad, head_mix, preferred_element_type=jnp.float32
    )[..., None]
    grad_scores = (attention * (grad_probs - row_dot) * score_factor).astype(jnp.bfloat16)
    grad_query = (
        jnp.einsum("chqk,ckhd->cqhd", grad_scores, key_heads, preferred_element_type=jnp.float32)
        .astype(jnp.bfloat16)
        .reshape(token_count, head_width)
    )
    grad_keys = (
        jnp.einsum("chqk,cqhd->ckhd", grad_scores, query_heads, preferred_element_type=jnp.float32)
        .astype(jnp.bfloat16)
        .reshape(pair_count * NLEN, head_width)
    )
    grad_values = (
        jnp.einsum(
            "chqk,cqhd->ckhd", attention_b, mix_heads_grad, preferred_element_type=jnp.float32
        )
        .astype(jnp.bfloat16)
        .reshape(pair_count * NLEN, head_width)
    )
    weight_parts = jnp.concatenate(
        [
            contract_first(normed, grad_query),
            contract_first(enc_rows, jnp.concatenate([grad_keys, grad_values], axis=1)),
            contract_first(grad_resid, mix_rows),
        ],
        axis=1,
    ).astype(jnp.bfloat16)
    summed = lax.psum_scatter(
        weight_parts, DATA, scatter_dimension=0, tiled=True
    ).astype(jnp.float32)
    query_grad = summed[:, :head_width]
    key_grad = summed[:, head_width : 2 * head_width]
    value_grad = summed[:, 2 * head_width : 3 * head_width]
    mix_grad = summed[:, 3 * head_width :].T
    activated, grad_query, _ = lax.optimization_barrier((activated, grad_query, weight_parts))
    ffn_part = contract_last(activated, down_turned)
    input_part = contract_last(grad_query, query_weight)
    layer_out = (resid_f + scatter_sum(ffn_part, PLANE)).astype(jnp.bfloat16)
    input_rows = scatter_sum(input_part, PLANE)
    grad_tokens = (
        grad_resid_rows.astype(jnp.float32) + norm_back(token_rows, base_rows, input_rows)
    ).astype(jnp.bfloat16)
    return (layer_out, grad_tokens, query_grad, key_grad, value_grad, mix_grad)


def solution(mesh):
    mesh = jax.sharding.Mesh(
        mesh.devices.reshape(-1, 2, SIDE, SIDE), DATA + PLANE
    )
    in_specs = (
        P(DATA, None),
        P(DATA, None, PLANE),
        P(DATA, None),
        P(DATA, None),
        P(None, PLANE),
        P(None, PLANE),
        P(None, PLANE),
        P(PLANE, None),
        P(DATA, PLANE),
        P(PLANE, DATA),
        P(DATA, None),
    )
    out_specs = (
        P(DATA + PLANE, None),
        P(DATA + PLANE, None),
        P(DATA, PLANE),
        P(DATA, PLANE),
        P(DATA, PLANE),
        P(PLANE, DATA),
    )
    return jax.shard_map(local, mesh=mesh, in_specs=in_specs, out_specs=out_specs, check_vma=False)
```

```python
import math

import jax
import jax.numpy as jnp
from jax import lax
from jax.sharding import PartitionSpec as P

HD = 128
BLOCK = 64
NLEN = 128
SIDE = 4
DATA = ("z", "core")
PLANE = ("y", "x")


epsilon = 1e-06
gelu_root = 0.7978845608028654
gelu_cubic = 0.044715


def rms_scale(values):
    return lax.rsqrt(jnp.mean(values * values, axis=-1, keepdims=True) + epsilon)


def norm_back(values, factor, incoming):
    normal_part = values * factor
    return (
        incoming - normal_part * jnp.mean(incoming * normal_part, axis=-1, keepdims=True)
    ) * factor


def gelu_value(inputs):
    inner = gelu_root * (inputs + gelu_cubic * inputs * inputs * inputs)
    return 0.5 * inputs * (1.0 + jnp.tanh(inner))


def gelu_slope(inputs):
    inner = gelu_root * (inputs + gelu_cubic * inputs * inputs * inputs)
    tanh_part = jnp.tanh(inner)
    return 0.5 * (1.0 + tanh_part) + 0.5 * inputs * (1.0 - tanh_part * tanh_part) * gelu_root * (
        1.0 + 3.0 * gelu_cubic * inputs * inputs
    )


def rounded(partial_value):
    return lax.optimization_barrier(partial_value.astype(jnp.bfloat16)).astype(jnp.float32)


def contract_last(left_side, right_side):
    return lax.dot_general(
        left_side, right_side, (((1,), (1,)), ((), ())), preferred_element_type=jnp.float32
    )


def contract_first(left_side, right_side):
    return lax.dot_general(
        left_side, right_side, (((0,), (0,)), ((), ())), preferred_element_type=jnp.float32
    )


def ring_shift(piece, axis, step):
    return lax.ppermute(
        piece, axis, [(place, (place + step) % SIDE) for place in range(SIDE)]
    )


def ring_gather(piece, axis, split_axis):
    here = lax.axis_index(axis)
    from_prev = ring_shift(piece, axis, 1)
    from_next = ring_shift(piece, axis, -1)
    half = piece.shape[split_axis] // 2
    first = lax.slice_in_dim(from_prev, 0, half, axis=split_axis)
    second = lax.slice_in_dim(from_next, half, 2 * half, axis=split_axis)
    opposite = jnp.concatenate(
        [ring_shift(first, axis, 1), ring_shift(second, axis, -1)], axis=split_axis
    )
    stacked = jnp.zeros((SIDE,) + piece.shape, piece.dtype)
    for shift, part in ((0, piece), (-1, from_prev), (1, from_next), (2, opposite)):
        stacked = lax.dynamic_update_index_in_dim(
            stacked, part, lax.rem(here + shift + SIDE, SIDE), 0
        )
    return stacked


def plane_gather(piece, halve_axis, split_axis):
    half = piece.shape[halve_axis] // 2
    first = lax.slice_in_dim(piece, 0, half, axis=halve_axis)
    second = lax.slice_in_dim(piece, half, 2 * half, axis=halve_axis)
    first = ring_gather(first, "x", split_axis)
    second = ring_gather(second, "y", split_axis)
    first = ring_gather(first, "y", split_axis + 1)
    second = ring_gather(second, "x", split_axis + 1)
    return first, jnp.swapaxes(second, 0, 1)


def gather_rows(rows):
    first, second = plane_gather(rows, 1, 1)
    count = SIDE * SIDE * rows.shape[0]
    half = rows.shape[1] // 2
    return jnp.concatenate([first.reshape(count, half), second.reshape(count, half)], axis=1)


def copies_to(rows, axis):
    size = lax.axis_size(axis)
    copies = jnp.broadcast_to(rows[None], (size,) + rows.shape)
    gathered = lax.all_to_all(copies, axis, split_axis=0, concat_axis=0, tiled=True)
    return gathered.reshape(size * rows.shape[0], rows.shape[1])


def scatter_sum(partial_rows, axis):
    size = lax.axis_size(axis)
    share = partial_rows.shape[0] // size
    swapped = lax.all_to_all(
        partial_rows.astype(jnp.bfloat16).reshape(size, share, partial_rows.shape[1]),
        axis,
        split_axis=0,
        concat_axis=0,
        tiled=True,
    )
    return jnp.sum(swapped.astype(jnp.float32), axis=0)


def local(
    tokens,
    neighbour_buffer,
    shard_ids,
    row_ids,
    query_weight,
    key_weight,
    value_weight,
    output_weight,
    up_weight,
    down_weight,
    grad_output,
):
    data_size = lax.axis_size(DATA)
    tensor_size = lax.axis_size(PLANE)
    token_count = tokens.shape[0]
    width = tokens.shape[1]
    block_count = shard_ids.shape[0]
    capacity = block_count // 2
    pair_count = 2 * block_count
    owners = shard_ids.reshape(pair_count)
    wanted = row_ids.reshape(pair_count)
    same_owner = owners[:, None] == owners[None, :]
    earlier = lax.broadcasted_iota(jnp.int32, (pair_count, pair_count), 0) < lax.broadcasted_iota(
        jnp.int32, (pair_count, pair_count), 1
    )
    slot_index = jnp.sum((same_owner & earlier).astype(jnp.int32), axis=0)
    owner_grid = lax.broadcasted_iota(jnp.int32, (data_size, capacity, pair_count), 0)
    slot_grid = lax.broadcasted_iota(jnp.int32, (data_size, capacity, pair_count), 1)
    slot_match = (owners[None, None, :] == owner_grid) & (slot_index[None, None, :] == slot_grid)
    requests = jnp.sum(jnp.where(slot_match, wanted[None, None, :], 0), axis=2)
    asked = lax.all_to_all(requests, DATA, split_axis=0, concat_axis=0, tiled=True)
    replies = lax.all_to_all(
        jnp.take(neighbour_buffer, asked, axis=0, mode="clip"),
        DATA,
        split_axis=0,
        concat_axis=0,
        tiled=True,
    )
    reply_rows = replies.reshape(data_size * capacity, replies.shape[2], replies.shape[3])
    local_enc = jnp.take(reply_rows, owners * capacity + slot_index, axis=0, mode="clip")
    frozen = jnp.concatenate([up_weight, down_weight.T], axis=1)
    local_enc, frozen = lax.optimization_barrier((local_enc, frozen))
    frozen_full = lax.all_gather(frozen, DATA, axis=0, tiled=True)
    hidden = up_weight.shape[1]
    up_full = frozen_full[:, :hidden]
    down_turned = frozen_full[:, hidden:]
    enc_a, enc_b = plane_gather(local_enc.reshape(pair_count * NLEN, width // tensor_size), 0, 0)
    half_rows = pair_count * NLEN // 2
    enc_rows = jnp.concatenate(
        [
            enc_a.transpose(2, 0, 1, 3).reshape(half_rows, width),
            enc_b.transpose(2, 0, 1, 3).reshape(half_rows, width),
        ],
        axis=0,
    )
    token_f = tokens.astype(jnp.float32)
    base_scale = rms_scale(token_f)
    normed = (token_f * base_scale).astype(jnp.bfloat16)
    query_rows = jnp.dot(normed, query_weight, preferred_element_type=jnp.float32).astype(
        jnp.bfloat16
    )
    head_width = query_rows.shape[1]
    both_weights = jnp.concatenate([key_weight, value_weight], axis=1)
    both_rows = jnp.dot(enc_rows, both_weights, preferred_element_type=jnp.float32).astype(
        jnp.bfloat16
    )
    key_rows = both_rows[:, :head_width]
    value_rows = both_rows[:, head_width:]
    heads_here = head_width // HD
    query_heads = query_rows.reshape(block_count, BLOCK, heads_here, HD)
    key_heads = key_rows.reshape(block_count, 2 * NLEN, heads_here, HD)
    value_heads = value_rows.reshape(block_count, 2 * NLEN, heads_here, HD)
    score_factor = 1.0 / math.sqrt(HD)
    scores = (
        jnp.einsum("cqhd,ckhd->chqk", query_heads, key_heads, preferred_element_type=jnp.float32)
        * score_factor
    )
    raised = jnp.exp(scores)
    attention = raised / jnp.sum(raised, axis=-1, keepdims=True)
    attention_b = attention.astype(jnp.bfloat16)
    head_mix = jnp.einsum(
        "chqk,ckhd->cqhd", attention_b, value_heads, preferred_element_type=jnp.float32
    ).astype(jnp.bfloat16)
    mix_rows = head_mix.reshape(token_count, head_width)
    attn_part = jnp.dot(mix_rows, output_weight, preferred_element_type=jnp.float32)
    rows_share = token_count // tensor_size
    row_start = lax.axis_index(PLANE) * rows_share
    token_rows = lax.dynamic_slice_in_dim(token_f, row_start, rows_share, 0)
    base_rows = lax.dynamic_slice_in_dim(base_scale, row_start, rows_share, 0)
    attn_rows = scatter_sum(attn_part, PLANE)
    resid_f = rounded(token_rows + attn_rows)
    resid_scale = rms_scale(resid_f)
    ffn_in = copies_to((resid_f * resid_scale).astype(jnp.bfloat16), PLANE)
    grad_act = lax.optimization_barrier(
        jnp.dot(grad_output, down_turned, preferred_element_type=jnp.float32)
    )
    pre_act = jnp.dot(ffn_in, up_full, preferred_element_type=jnp.float32)
    activated = gelu_value(pre_act).astype(jnp.bfloat16)
    grad_pre = (grad_act * gelu_slope(pre_act)).astype(jnp.bfloat16)
    norm_part = contract_last(grad_pre, up_full)
    norm_rows = scatter_sum(norm_part, PLANE)
    out_rows = lax.dynamic_slice_in_dim(grad_output, row_start, rows_share, 0).astype(jnp.float32)
    grad_resid_rows = (out_rows + norm_back(resid_f, resid_scale, norm_rows)).astype(jnp.bfloat16)
    grad_resid = gather_rows(grad_resid_rows)
    grad_mix = contract_last(grad_resid, output_weight).astype(jnp.bfloat16)
    mix_heads_grad = grad_mix.reshape(block_count, BLOCK, heads_here, HD)
    grad_probs = jnp.einsum(
        "cqhd,ckhd->chqk", mix_heads_grad, value_heads, preferred_element_type=jnp.float32
    )
    row_dot = jnp.einsum(
        "cqhd,cqhd->chq", mix_heads_grad, head_mix, preferred_element_type=jnp.float32
    )[..., None]
    grad_scores = (attention * (grad_probs - row_dot) * score_factor).astype(jnp.bfloat16)
    grad_query = (
        jnp.einsum("chqk,ckhd->cqhd", grad_scores, key_heads, preferred_element_type=jnp.float32)
        .astype(jnp.bfloat16)
        .reshape(token_count, head_width)
    )
    grad_keys = (
        jnp.einsum("chqk,cqhd->ckhd", grad_scores, query_heads, preferred_element_type=jnp.float32)
        .astype(jnp.bfloat16)
        .reshape(pair_count * NLEN, head_width)
    )
    grad_values = (
        jnp.einsum(
            "chqk,cqhd->ckhd", attention_b, mix_heads_grad, preferred_element_type=jnp.float32
        )
        .astype(jnp.bfloat16)
        .reshape(pair_count * NLEN, head_width)
    )
    enc_grad = contract_first(enc_rows, jnp.concatenate([grad_keys, grad_values], axis=1))
    weight_parts = jnp.stack(
        [
            part.astype(jnp.bfloat16).reshape(data_size, -1, head_width)
            for part in (
                contract_first(normed, grad_query),
                enc_grad[:, :head_width],
                enc_grad[:, head_width:],
                contract_first(grad_resid, mix_rows),
            )
        ],
        axis=1,
    )
    summed = lax.psum_scatter(weight_parts, DATA, scatter_dimension=0, tiled=False).astype(
        jnp.float32
    )
    query_grad, key_grad, value_grad = summed[0], summed[1], summed[2]
    mix_grad = summed[3].T
    activated, grad_query, _ = lax.optimization_barrier((activated, grad_query, weight_parts))
    ffn_part = contract_last(activated, down_turned)
    input_part = contract_last(grad_query, query_weight)
    layer_out = (resid_f + scatter_sum(ffn_part, PLANE)).astype(jnp.bfloat16)
    input_rows = scatter_sum(input_part, PLANE)
    grad_tokens = (
        grad_resid_rows.astype(jnp.float32) + norm_back(token_rows, base_rows, input_rows)
    ).astype(jnp.bfloat16)
    return (layer_out, grad_tokens, query_grad, key_grad, value_grad, mix_grad)


def solution(mesh):
    mesh = jax.sharding.Mesh(
        mesh.devices.reshape(-1, 2, SIDE, SIDE), DATA + PLANE
    )
    in_specs = (
        P(DATA, None),
        P(DATA, None, PLANE),
        P(DATA, None),
        P(DATA, None),
        P(None, PLANE),
        P(None, PLANE),
        P(None, PLANE),
        P(PLANE, None),
        P(DATA, PLANE),
        P(PLANE, DATA),
        P(DATA, None),
    )
    out_specs = (
        P(DATA + PLANE, None),
        P(DATA + PLANE, None),
        P(DATA, PLANE),
        P(DATA, PLANE),
        P(DATA, PLANE),
        P(PLANE, DATA),
    )
    return jax.shard_map(local, mesh=mesh, in_specs=in_specs, out_specs=out_specs, check_vma=False)
```
